256 devices in a mesh: xy: 32 (over z, x_hi, core), gz: 8 (over x_lo, y).
Axes of the slice: x: 4 (x_hi: 2, x_lo: 2; x = x_hi * 2 + x_lo), y: 4, z: 8, core: 2. Of those that a mesh axis runs over, the one named last changes fastest.
Arguments:
- field_tiles: bfloat16 [32, 128, 128, 1024], P('xy', None, None, 'gz'), may hold values from -6 to 6
- core_x: bfloat16 [512, 192], replicated, may hold values from -0.25 to 0.25
- core_y: bfloat16 [1024, 192], replicated, may hold values from -0.1875 to 0.1875
- core_z: bfloat16 [1024, 192], P('gz'), may hold values from -0.1875 to 0.1875
- x_second: bfloat16 [512, 96], replicated, may hold values from -0.25 to 0.25
- x_third: bfloat16 [512, 96], replicated, may hold values from -0.25 to 0.25
- y_first: bfloat16 [1024, 96], replicated, may hold values from -0.1875 to 0.1875
- y_third: bfloat16 [1024, 96], replicated, may hold values from -0.1875 to 0.1875
- z_first: bfloat16 [1024, 96], P('gz'), may hold values from -0.1875 to 0.1875
- z_second: bfloat16 [1024, 96], P('gz'), may hold values from -0.1875 to 0.1875
Outputs:
- mode_one: float32 [512, 96], P(('xy', 'gz'))
- mode_two: float32 [1024, 96], P(('xy', 'gz'))
- mode_three: float32 [96, 1024], P('xy', 'gz')
- core_sketch: float32 [192, 192, 192], P('xy', None, 'gz')
The draws below stay inside these ranges and needn't reach their ends.
All inputs are finite; a program needn't handle non-finite values.
Results may differ from the reference program's by a relative error of at most 0.007.
Values may be sent and summed in bfloat16 or wider, within the bound.
A program may use at most 128 MiB of HBM per device.

```python
import jax
import jax.numpy as jnp
from jax import lax

K = 96
S = 192
TX = 128
TY = 128
NX = 512
NY = 1024
NZ = 1024
N_XY = 32


def block_scale(rng, extent, pieces, low, largest):
    factor_of = 1.0
    for dim, shards_of in pieces:
        steps = jax.random.uniform(jax.random.fold_in(jax.random.fold_in(rng, 6), dim), (shards_of,), jnp.float32, low / len(pieces), largest / len(pieces))
        factor_of = factor_of * jnp.repeat(jnp.exp(steps), extent[dim] // shards_of).reshape((-1,) + (1,) * (len(extent) - 1 - dim))
    return factor_of


def scatter_about(key, extent, spread, reach, cuts=(), kind=jnp.bfloat16):
    result = spread * jax.random.normal(key, extent, jnp.float32)
    if cuts:
        result = result * block_scale(key, extent, cuts, -0.22, 0.18)
    return jnp.clip(result, -reach, reach).astype(kind)


def setup_inputs(seed: int = 0) -> dict:
    streams_of = jax.random.split(jax.random.key(seed), 11)
    return {
        "field_tiles": scatter_about(streams_of[0], (N_XY, TX, TY, NZ), 1.0, 6.0, ((0, 32), (3, 8))),
        "core_x": scatter_about(streams_of[1], (NX, S), NX ** -0.5, 0.25),
        "core_y": scatter_about(streams_of[2], (NY, S), NY ** -0.5, 0.1875),
        "core_z": scatter_about(streams_of[3], (NZ, S), NZ ** -0.5, 0.1875, ((0, 8),)),
        "x_second": scatter_about(streams_of[4], (NX, K), NX ** -0.5, 0.25),
        "x_third": scatter_about(streams_of[5], (NX, K), NX ** -0.5, 0.25),
        "y_first": scatter_about(streams_of[6], (NY, K), NY ** -0.5, 0.1875),
        "y_third": scatter_about(streams_of[7], (NY, K), NY ** -0.5, 0.1875),
        "z_first": scatter_about(streams_of[8], (NZ, K), NZ ** -0.5, 0.1875, ((0, 8),)),
        "z_second": scatter_about(streams_of[9], (NZ, K), NZ ** -0.5, 0.1875, ((0, 8),)),
    }


def row_slice(matrix, offset, length):
    return lax.dynamic_slice_in_dim(matrix, offset, length, 0).astype(jnp.float32)


def reference(field_tiles, core_x, core_y, core_z, x_second, x_third, y_first, y_third, z_first, z_second):
    column_tiles = N_XY // 4
    z_pair = jnp.concatenate([z_first, z_second], axis=1).astype(jnp.float32)

    def one_tile(totals, tile_index):
        first_part, second_part, third_part, plane_sum = totals
        block_data = lax.dynamic_index_in_dim(field_tiles, tile_index, 0, keepdims=False).astype(jnp.float32)
        x_offset = ((tile_index // column_tiles) * TX).astype(jnp.int32)
        y_offset = ((tile_index % column_tiles) * TY).astype(jnp.int32)
        paired = jnp.einsum('abz,zk->abk', block_data, z_pair)
        g_one = jnp.sum(paired[:, :, :K] * row_slice(y_first, y_offset, TY)[None], axis=1)
        g_two = jnp.sum(paired[:, :, K:] * row_slice(x_second, x_offset, TX)[:, None], axis=0)
        across = jnp.einsum('abz,ak->bkz', block_data, row_slice(x_third, x_offset, TX))
        g_three = jnp.sum(across * row_slice(y_third, y_offset, TY)[:, :, None], axis=0)
        first_part = lax.dynamic_update_slice_in_dim(
            first_part, lax.dynamic_slice_in_dim(first_part, x_offset, TX, 0) + g_one, x_offset, 0)
        second_part = lax.dynamic_update_slice_in_dim(
            second_part, lax.dynamic_slice_in_dim(second_part, y_offset, TY, 0) + g_two, y_offset, 0)
        third_part = third_part + g_three
        lowered = jnp.einsum('abz,ap->pbz', block_data, row_slice(core_x, x_offset, TX)).astype(jnp.bfloat16)
        plane_sum = plane_sum + jnp.einsum('pbz,bq->pqz', lowered.astype(jnp.float32), row_slice(core_y, y_offset, TY))
        return (first_part, second_part, third_part, plane_sum), None

    start_totals = (jnp.zeros((NX, K), jnp.float32), jnp.zeros((NY, K), jnp.float32),
                    jnp.zeros((K, NZ), jnp.float32), jnp.zeros((S, S, NZ), jnp.float32))
    totals, _ = lax.scan(one_tile, start_totals, jnp.arange(N_XY, dtype=jnp.int32))
    mode_one, mode_two, mode_three, plane_sum = totals
    core_sketch = jnp.einsum('pqz,zr->pqr', plane_sum, core_z.astype(jnp.float32), precision=lax.Precision.HIGHEST)
    return mode_one, mode_two, mode_three, core_sketch
```

```python
import functools

import jax
import jax.numpy as jnp
import numpy as np
from jax import lax
from jax.experimental import pallas as pl
from jax.experimental.pallas import tpu as pltpu
from jax.sharding import PartitionSpec as P

MESH = pl.DeviceIdType.MESH
F32, BF16 = jnp.float32, jnp.bfloat16
K = 96
S = 192
T = 128
CH = 16
NCH = T // CH
ROWS = 9 * CH


def one_hot(rows, columns, pairs):
    m = np.zeros((rows, columns), np.float32)
    for r, c in pairs:
        m[r, c] = 1.0
    return m


def tables():
    r_of = lambda c, h, e, i: 24 * ((e // 4 % 2) * 4 + e % 4) + 12 * (e // 8) + 6 * c + 3 * h + i
    rsel = np.stack(
        [
            one_hot(96, S, [(h * 48 + e * 3 + i, r_of(c, h, e, i)) for h in range(2) for e in range(16) for i in range(3)])
            for c in range(2)
        ]
    )
    qsel = np.stack(
        [
            one_hot(S, 256, [(q, q) for q in range(S)]),
            one_hot(S, 256, [(q, q if q < 128 else q + 64) for q in range(S)]),
        ]
    )
    psel = one_hot(256, S, [(8 * t + i, 6 * t + i) for t in range(32) for i in range(6)])
    ksel = one_hot(256, K, [(8 * t + i, 3 * t + i) for t in range(32) for i in range(3)])
    zsel = np.stack([one_hot(K, 256, [(k, k) for k in range(K)]), one_hot(K, 256, [(k, 128 + k) for k in range(K)])])
    eye = one_hot(K, 128, [(k, k) for k in range(K)])
    return [jnp.asarray(m, BF16) for m in (rsel, qsel, psel, ksel, zsel, eye)]


def nn(a, b):
    return lax.dot_general(a, b, (((1,), (0,)), ((), ())), preferred_element_type=F32)


def nt(a, b):
    return lax.dot_general(a, b, (((1,), (1,)), ((), ())), preferred_element_type=F32)


def core_kernel(
    field, core_x, core_y, core_z, x_second, x_third, y_first, y_third, z_first, z_second,
    rsel, qsel, psel, ksel, zsel, eye,
    out, g1, g2,
    own, par, wt, us, send, mid, ring, second, gath, hbuf, zrecv, fbuf, frecv, wy, zp, g3,
    own_sem, par_s, par_r, mid_s, mid_r, dir_s, dir_r, com_s, com_r, sec_s, sec_r, z_s, z_r, f_s, f_r,
):
    t, g = lax.axis_index("xy"), lax.axis_index("gz")
    z, s = lax.div(t, 4), lax.rem(t, 4)
    xh, c = lax.div(s, 2), lax.rem(s, 2)
    xl, y = lax.div(g, 4), lax.rem(g, 4)
    X = xh * 2 + xl
    u, v = lax.div(t, 8), lax.rem(t, 8)
    mate = t + 1 - 2 * c

    def ring_dev(d, q):
        tt = t + (1 - d) * 2 * (lax.div(q, 2) - xh)
        gg = g + (1 - d) * 4 * (lax.rem(q, 2) - xl) + d * (q - y)
        return (tt, gg)

    def place(d):
        return (1 - d) * X + d * y

    def step(p, k):
        return lax.rem(p + k, 4)

    def copy(src, dst, ss, rs, dev):
        return pltpu.make_async_remote_copy(
            src_ref=src, dst_ref=dst, send_sem=ss, recv_sem=rs, device_id=dev, device_id_type=MESH
        )

    def own_copy(ch):
        return pltpu.make_async_copy(field.at[0, pl.ds(ch * CH, CH)], own.at[ch], own_sem.at[ch])

    def par_copy(ch):
        return copy(field.at[0, pl.ds(ch * CH, CH)], par.at[ch], par_s.at[ch], par_r.at[ch], (mate, g))

    def mid_copy(ch, w):
        d = lax.rem(ch, 2)
        p = place(d)
        src = send.at[ch, pl.ds(step(p, 2) * 4 + 2 * w, 2)]
        return copy(src, mid.at[ch, w], mid_s.at[ch, w], mid_r.at[ch, w], ring_dev(d, step(p, 1 + 2 * w)))

    def part(ch, w, h):
        p = place(lax.rem(ch, 2))
        return send.at[ch, pl.ds(step(p, 1 + 2 * w) * 4 + 2 * h, 2)]

    def dir_copy(ch, w):
        d = lax.rem(ch, 2)
        dst = ring.at[ch, w, pl.ds(2 * (1 - w), 2)]
        return copy(part(ch, w, 1 - w), dst, dir_s.at[ch, w], dir_r.at[ch, w], ring_dev(d, step(place(d), 1 + 2 * w)))

    def com_copy(ch, w):
        d = lax.rem(ch, 2)
        dst = ring.at[ch, w, pl.ds(2 * w, 2)]
        return copy(part(ch, w, w), dst, com_s.at[ch, w], com_r.at[ch, w], ring_dev(d, step(place(d), 1 + 2 * w)))

    def sec_copy(ch, k):
        d = lax.rem(ch, 2)
        q = step(place(1 - d), k)
        src = send.at[ch, place(d) * 4 + q]
        return copy(src, second.at[ch, k - 1], sec_s.at[ch, k - 1], sec_r.at[ch, k - 1], ring_dev(1 - d, q))

    def z_copy(k):
        zz = lax.rem(z + k, 8)
        return copy(hbuf.at[zz], zrecv.at[k - 1], z_s.at[k - 1], z_r.at[k - 1], (zz * 4 + s, g))

    def f_copy(k):
        q = step(s, k)
        return copy(fbuf.at[q], frecv.at[k - 1], f_s.at[k - 1], f_r.at[k - 1], (z * 4 + q, g))

    def start_own(ch, _):
        own_copy(ch).start()
        return 0

    lax.fori_loop(0, NCH, start_own, 0)

    barrier = pltpu.get_barrier_semaphore()
    others = [ring_dev(0, step(X, 1)), ring_dev(0, step(X, 3))]
    others += [ring_dev(1, step(y, k)) for k in (1, 2, 3)]
    others += [(lax.rem(z + k, 8) * 4 + s, g) for k in range(1, 8)]
    others += [(z * 4 + step(s, k), g) for k in (1, 2, 3)]
    for dev in others:
        pl.semaphore_signal(barrier, inc=1, device_id=dev, device_id_type=MESH)
    pl.semaphore_wait(barrier, len(others))

    def start_par(ch, _):
        par_copy(ch).start()
        return 0

    lax.fori_loop(0, NCH, start_par, 0)

    def rows(ref, base, n=T):
        return ref[pl.ds(pl.multiple_of(base, n), n), :]

    czt = nt(rsel[c], core_z[...]).astype(BF16)
    for h in range(2):
        wy[h, 0:T, :] = nn(rows(core_y, v * T), qsel[h]).astype(BF16)
        wy[h, T : 2 * T, :] = nn(rows(core_y, (v + 1 - 2 * c) * T), qsel[h]).astype(BF16)
    zp[...] = (nn(z_first[...], zsel[0]) + nn(z_second[...], zsel[1])).astype(BF16)
    y1 = nn(rows(y_first, v * T), eye[...])
    y3 = nt(eye[:, 0:K], rows(y_third, v * T))
    g2[...] = jnp.zeros_like(g2)
    g3[...] = jnp.zeros_like(g3)

    def contract(ch):
        own_copy(ch).wait()
        par_copy(ch).wait_recv()
        for a in range(CH):
            both = jnp.concatenate([own[ch, a], par[ch, a]], axis=0)
            w = nt(czt, both).astype(BF16)
            wt[0, a * 48 : a * 48 + 48, :] = w[0:48]
            wt[1, a * 48 : a * 48 + 48, :] = w[48:96]
        for b in range(4):
            top = nn(wt[0, b * 192 : b * 192 + 192, :], wy[0])
            bot = nn(wt[1, b * 192 : b * 192 + 192, :], wy[1])
            rest = top[:, 128:] + bot[:, 128:]
            for a in range(4):
                at = (b * 4 + a) * ROWS
                us[at : at + 48, :] = top[a * 48 : a * 48 + 48, 0:128]
                us[at + 48 : at + 96, :] = bot[a * 48 : a * 48 + 48, 0:128]
                us[at + 96 : at + 144, :] = rest[a * 48 : a * 48 + 48]
        d = lax.rem(ch, 2)

        def reorder(e, _):
            q = (1 - d) * e + d * (lax.rem(e, 4) * 4 + lax.div(e, 4))
            for kind in range(3):
                for i in range(3):
                    j = kind * 3 + i
                    block = us[pl.ds(kind * 48 + i + e * 3, CH, stride=ROWS), :]
                    send[ch, q, j * CH : j * CH + CH, :] = block.astype(BF16)
            return 0

        lax.fori_loop(0, 16, reorder, 0, unroll=True)
        for w in range(2):
            mid_copy(ch, w).start()
            dir_copy(ch, w).start()

    def modes(ch):
        x2 = nn(rows(x_second, u * T + ch * CH, CH), eye[...])
        x3 = nt(eye[:, 0:K], rows(x_third, u * T + ch * CH, CH))
        total = g2[...]
        factors = []
        for a in range(CH):
            m = nn(own[ch, a], zp[...])
            g1[pl.ds(ch * CH + a, 1), :] = jnp.sum(m[:, 0:128] * y1, axis=0, keepdims=True)
            total = total + m[:, 128:] * x2[a : a + 1]
            factors.append((y3 * x3[:, a : a + 1]).astype(BF16))
        g2[...] = total
        g3[...] += nn(jnp.concatenate(factors, axis=1), own[ch].reshape(CH * T, T))

    def forward(ch):
        p = place(lax.rem(ch, 2))
        for w in range(2):
            mid_copy(ch, w).wait_recv()
            base = step(p, 1 + 2 * w) * 4 + 2 * w
            for h in range(2):
                mine = send[ch, base + h].astype(F32)
                send[ch, base + h] = (mine + mid[ch, w, h].astype(F32)).astype(BF16)
            com_copy(ch, w).start()

    def finish(ch):
        p = place(lax.rem(ch, 2))
        for w in range(2):
            dir_copy(ch, w).wait_recv()
            com_copy(ch, w).wait_recv()
        for b in range(4):
            tot = send[ch, p * 4 + b].astype(F32) + ring[ch, 0, b].astype(F32) + ring[ch, 1, b].astype(F32)
            send[ch, p * 4 + b] = tot.astype(BF16)
        for k in (1, 2, 3):
            sec_copy(ch, k).start()

    def turn(it, _):
        @pl.when(it < NCH)
        def _():
            contract(it)

        @pl.when((it >= 1) & (it < NCH + 1))
        def _():
            forward(it - 1)

        @pl.when(it < NCH)
        def _():
            modes(it)

        @pl.when(it >= 2)
        def _():
            finish(it - 2)

        return 0

    lax.fori_loop(0, NCH + 2, turn, 0)

    def collect(ch, _):
        d = lax.rem(ch, 2)
        for k in (1, 2, 3):
            sec_copy(ch, k).wait_recv()
        tot = send[ch, place(d) * 4 + place(1 - d)].astype(F32)
        for k in range(3):
            tot = tot + second[ch, k].astype(F32)
        tot = tot.astype(BF16)
        for j in range(9):
            gath[j, pl.ds(pl.multiple_of(ch * CH, CH), CH), :] = tot[j * CH : j * CH + CH]
        return 0

    lax.fori_loop(0, NCH, collect, 0)

    cxp = nt(psel[...], rows(core_x, u * T)).astype(BF16)
    for j in range(10):
        if j < 9:
            piece = nn(cxp, gath[j])
        else:
            piece = nn(ksel[...], g3[...].astype(BF16))
        hbuf[:, j * 32 : j * 32 + 32, :] = piece.astype(BF16).reshape(8, 32, T)
    for k in range(1, 8):
        z_copy(k).start()
    for k in range(1, 8):
        z_copy(k).wait_recv()
    for j in range(10):
        tot = hbuf[z, j * 32 : j * 32 + 32, :].astype(F32)
        for k in range(7):
            tot = tot + zrecv[k, j * 32 : j * 32 + 32, :].astype(F32)
        fbuf[:, j] = tot.reshape(4, 8, T)
    for k in (1, 2, 3):
        f_copy(k).start()
    out[s] = fbuf[s]
    for k in (1, 2, 3):
        f_copy(k).wait_recv()
        out[step(s, 4 - k)] = frecv[k - 1]

    def drain(ch, _):
        par_copy(ch).wait_send()
        for w in range(2):
            mid_copy(ch, w).wait_send()
            dir_copy(ch, w).wait_send()
            com_copy(ch, w).wait_send()
        for k in (1, 2, 3):
            sec_copy(ch, k).wait_send()
        return 0

    lax.fori_loop(0, NCH, drain, 0)
    for k in range(1, 8):
        z_copy(k).wait_send()
    for k in (1, 2, 3):
        f_copy(k).wait_send()


def mode_kernel(m, sel, one, two, recv, msg, r1, r2, a_s, a_r, b_s, b_r, c_s, c_r):
    t, g = lax.axis_index("xy"), lax.axis_index("gz")
    u, v = lax.div(t, 8), lax.rem(t, 8)

    def copy(src, dst, ss, rs, dev):
        return pltpu.make_async_remote_copy(
            src_ref=src, dst_ref=dst, send_sem=ss, recv_sem=rs, device_id=dev, device_id_type=MESH
        )

    def a_copy(k):
        q = lax.rem(g + k, 8)
        return copy(m.at[q], recv.at[k - 1], a_s.at[k - 1], a_r.at[k - 1], (t, q))

    def b_copy(k):
        q = lax.rem(v + k, 8)
        return copy(msg.at[q], r1.at[k - 1], b_s.at[k - 1], b_r.at[k - 1], (u * 8 + q, g))

    def c_send(b):
        return copy(msg.at[8 + b], r2.at[u], c_s.at[b], c_r.at[u], (v * 4 + b, g))

    def c_recv(k):
        return copy(msg.at[8], r2.at[k], c_s.at[0], c_r.at[k], (k * 8 + lax.div(t, 4), g))

    barrier = pltpu.get_barrier_semaphore()
    for k in range(1, 8):
        pl.semaphore_signal(barrier, inc=1, device_id=(t, lax.rem(g + k, 8)), device_id_type=MESH)
        pl.semaphore_signal(barrier, inc=1, device_id=(u * 8 + lax.rem(v + k, 8), g), device_id_type=MESH)
    for k in range(4):
        source = k * 8 + lax.div(t, 4)

        @pl.when(source != t)
        def _():
            pl.semaphore_signal(barrier, inc=1, device_id=(source, g), device_id_type=MESH)

    @pl.when(lax.div(t, 4) == v)
    def _():
        pl.semaphore_wait(barrier, 17)

    @pl.when(lax.div(t, 4) != v)
    def _():
        pl.semaphore_wait(barrier, 18)

    for k in range(1, 8):
        a_copy(k).start()
    total = m[g]
    for k in range(1, 8):
        a_copy(k).wait_recv()
        total = total + recv[k - 1]
    spread = lax.dot_general(
        sel[...], total, (((1,), (0,)), ((), ())), preferred_element_type=F32, precision=lax.Precision.HIGHEST
    )
    msg[...] = spread.reshape(12, 8, 128)
    for k in range(1, 8):
        b_copy(k).start()
    for b in range(4):

        @pl.when(v * 4 + b != t)
        def _():
            c_send(b).start()

        @pl.when(v * 4 + b == t)
        def _():
            r2[u] = msg[8 + b]

    first = msg[v]
    for k in range(1, 8):
        b_copy(k).wait_recv()
        first = first + r1[k - 1]
    one[...] = first
    for k in range(4):

        @pl.when(k * 8 + lax.div(t, 4) != t)
        def _():
            c_recv(k).wait_recv()

    two[...] = r2[0] + r2[1] + r2[2] + r2[3]
    for k in range(1, 8):
        a_copy(k).wait_send()
        b_copy(k).wait_send()
    for b in range(4):

        @pl.when(v * 4 + b != t)
        def _():
            c_send(b).wait_send()


def shards(*args):
    vm = pl.BlockSpec(memory_space=pltpu.VMEM)
    dma = pltpu.SemaphoreType.DMA
    out, g1, g2 = pl.pallas_call(
        core_kernel,
        out_shape=(
            jax.ShapeDtypeStruct((4, 10, 8, 128), F32),
            jax.ShapeDtypeStruct((T, 128), F32),
            jax.ShapeDtypeStruct((T, 128), F32),
        ),
        in_specs=[pl.BlockSpec(memory_space=pl.ANY)] + [vm] * 15,
        out_specs=(vm, vm, vm),
        scratch_shapes=[
            pltpu.VMEM((NCH, CH, T, T), BF16),
            pltpu.VMEM((NCH, CH, T, T), BF16),
            pltpu.VMEM((2, CH * 48, 256), BF16),
            pltpu.VMEM((CH * ROWS, 128), F32),
            pltpu.VMEM((NCH, 16, ROWS, 128), BF16),
            pltpu.VMEM((NCH, 2, 2, ROWS, 128), BF16),
            pltpu.VMEM((NCH, 2, 4, ROWS, 128), BF16),
            pltpu.VMEM((NCH, 3, ROWS, 128), BF16),
            pltpu.VMEM((9, T, 128), BF16),
            pltpu.VMEM((8, 320, 128), BF16),
            pltpu.VMEM((7, 320, 128), BF16),
            pltpu.VMEM((4, 10, 8, 128), F32),
            pltpu.VMEM((3, 10, 8, 128), F32),
            pltpu.VMEM((2, 2 * T, 256), BF16),
            pltpu.VMEM((T, 256), BF16),
            pltpu.VMEM((K, T), F32),
            dma((NCH,)), dma((NCH,)), dma((NCH,)),
            dma((NCH, 2)), dma((NCH, 2)), dma((NCH, 2)), dma((NCH, 2)), dma((NCH, 2)), dma((NCH, 2)),
            dma((NCH, 3)), dma((NCH, 3)), dma((7,)), dma((7,)), dma((3,)), dma((3,)),
        ],
        compiler_params=pltpu.CompilerParams(
            collective_id=0, has_side_effects=True, vmem_limit_bytes=56 * 1024 * 1024
        ),
    )(*args, *tables())

    first = g1.reshape(8, 8, 2, 128).transpose(1, 0, 2, 3).reshape(8, 16, 128)
    two = g2.reshape(4, 8, 4, 128).transpose(1, 0, 2, 3).reshape(8, 16, 128)
    sel = one_hot(96, 32, [(8 * h + i, 2 * h + i) for h in range(8) for i in range(2)]
                  + [(64 + 8 * h + i, 16 + 4 * h + i) for h in range(4) for i in range(4)])
    mode_one, mode_two = pl.pallas_call(
        mode_kernel,
        out_shape=(jax.ShapeDtypeStruct((8, 128), F32), jax.ShapeDtypeStruct((8, 128), F32)),
        in_specs=[vm, vm],
        out_specs=(vm, vm),
        scratch_shapes=[
            pltpu.VMEM((7, 32, 128), F32),
            pltpu.VMEM((12, 8, 128), F32),
            pltpu.VMEM((7, 8, 128), F32),
            pltpu.VMEM((4, 8, 128), F32),
            dma((7,)), dma((7,)), dma((7,)), dma((7,)), dma((4,)), dma((4,)),
        ],
        compiler_params=pltpu.CompilerParams(collective_id=1, has_side_effects=True),
    )(jnp.concatenate([first, two], axis=1), jnp.asarray(sel, F32))

    mode_three = jnp.sum(out[:, 9, 0:3], axis=0)
    core = out[:, 0:9].reshape(4, 3, 3, 8, 128)[:, :, :, 0:6]
    low = core[:, 0:2].transpose(3, 4, 0, 1, 2).reshape(6, 128, 24)
    high = core[:, 2].reshape(4, 3, 6, 2, 64).transpose(2, 4, 0, 3, 1).reshape(6, 64, 24)
    core_sketch = jnp.concatenate([low, high], axis=1)
    return (mode_one[0:2, 0:K], mode_two[0:4, 0:K], mode_three, core_sketch)


def solution(mesh):
    return jax.shard_map(
        shards,
        mesh=mesh,
        in_specs=(
            P("xy", None, None, "gz"),
            P(), P(), P("gz", None), P(), P(), P(), P(), P("gz", None), P("gz", None),
        ),
        out_specs=(
            P(("xy", "gz"), None),
            P(("xy", "gz"), None),
            P("xy", "gz"),
            P("xy", None, "gz"),
        ),
        check_vma=False,
    )
```

```python
import jax
import jax.numpy as jnp
from jax import lax
from jax.experimental import pallas as pl
from jax.experimental.pallas import tpu as pltpu
from jax.sharding import PartitionSpec as P

MESH = pl.DeviceIdType.MESH
F32, BF16, I32 = jnp.float32, jnp.bfloat16, jnp.int32
K = 96
S = 192
T = 128
CH = 32
NCH = T // CH
PARTS = 3
UNITS = PARTS * NCH
ROWS = 3 * CH
MODE = 16
FORWARD, FINISH, COLLECT, ZLAG = 1, 2, 4, 2
MODE_A, MODE_B = 8, 11


def nn(a, b, precision=None):
    return lax.dot_general(a, b, (((1,), (0,)), ((), ())), preferred_element_type=F32, precision=precision)


def nt(a, b):
    return lax.dot_general(a, b, (((1,), (1,)), ((), ())), preferred_element_type=F32)


def pick(rows, columns, column_of, dtype=BF16):
    r = lax.broadcasted_iota(I32, (rows, columns), 0)
    return jnp.where(lax.broadcasted_iota(I32, (rows, columns), 1) == column_of(r), 1.0, 0.0).astype(dtype)


def main_kernel(
    field, core_x, core_y, core_z, x_second, x_third, y_first, y_third, z_first, z_second,
    out,
    own, par, wt, us, send, mid, ring, second, gath, hbuf, zrecv, fbuf, frecv,
    cx, cy, cz, tx2, tx3, ty1, ty3, tz1, tz2,
    czt, cxp, wy, zp, y1, x2, x3, g1, g2, g3, m12, arecv, msg, r1, r2,
    in_s, own_sem, par_s, par_r, mid_s, mid_r, dir_s, dir_r, com_s, com_r, sec_s, sec_r, z_s, z_r, f_s, f_r,
    ma_s, ma_r, mb_s, mb_r, mc_s, mc_r,
):
    t, g = lax.axis_index("xy"), lax.axis_index("gz")
    z, s = lax.div(t, 4), lax.rem(t, 4)
    xh, c = lax.div(s, 2), lax.rem(s, 2)
    xl, y = lax.div(g, 4), lax.rem(g, 4)
    X = xh * 2 + xl
    u, v = lax.div(t, 8), lax.rem(t, 8)
    mate = t + 1 - 2 * c

    def ring_dev(d, q):
        tt = t + (1 - d) * 2 * (lax.div(q, 2) - xh)
        gg = g + (1 - d) * 4 * (lax.rem(q, 2) - xl) + d * (q - y)
        return (tt, gg)

    def place(d):
        return (1 - d) * X + d * y

    def step(p, k):
        return lax.rem(p + k, 4)

    def copy(src, dst, ss, rs, dev):
        return pltpu.make_async_remote_copy(
            src_ref=src, dst_ref=dst, send_sem=ss, recv_sem=rs, device_id=dev, device_id_type=MESH
        )

    def own_copy(ch):
        return pltpu.make_async_copy(field.at[0, pl.ds(ch * CH, CH)], own.at[ch], own_sem.at[ch])

    def par_copy(ch):
        return copy(field.at[0, pl.ds(ch * CH, CH)], par.at[ch], par_s.at[ch], par_r.at[ch], (mate, g))

    def mid_copy(n, w):
        d = lax.rem(n, 2)
        p = place(d)
        src = send.at[n, pl.ds(step(p, 2) * 4 + 2 * w, 2)]
        return copy(src, mid.at[n, w], mid_s.at[n, w], mid_r.at[n, w], ring_dev(d, step(p, 1 + 2 * w)))

    def part(n, w, h):
        p = place(lax.rem(n, 2))
        return send.at[n, pl.ds(step(p, 1 + 2 * w) * 4 + 2 * h, 2)]

    def dir_copy(n, w):
        d = lax.rem(n, 2)
        dst = ring.at[n, w, pl.ds(2 * (1 - w), 2)]
        return copy(part(n, w, 1 - w), dst, dir_s.at[n, w], dir_r.at[n, w], ring_dev(d, step(place(d), 1 + 2 * w)))

    def com_copy(n, w):
        d = lax.rem(n, 2)
        dst = ring.at[n, w, pl.ds(2 * w, 2)]
        return copy(part(n, w, w), dst, com_s.at[n, w], com_r.at[n, w], ring_dev(d, step(place(d), 1 + 2 * w)))

    def sec_copy(n, k):
        d = lax.rem(n, 2)
        q = step(place(1 - d), k)
        src = send.at[n, place(d) * 4 + q]
        return copy(src, second.at[n, k - 1], sec_s.at[n, k - 1], sec_r.at[n, k - 1], ring_dev(1 - d, q))

    def z_copy(i, k):
        zz = lax.rem(z + k, 8)
        size = 128 if i == 1 else 96
        src, dst = hbuf.at[i, zz, pl.ds(0, size)], zrecv.at[i, k - 1, pl.ds(0, size)]
        return copy(src, dst, z_s.at[i, k - 1], z_r.at[i, k - 1], (zz * 4 + s, g))

    def f_copy(i, k):
        q = step(s, k)
        size = 4 if i == 1 else 3
        src, dst = fbuf.at[i, q, pl.ds(0, size)], frecv.at[i, k - 1, pl.ds(0, size)]
        return copy(src, dst, f_s.at[i, k - 1], f_r.at[i, k - 1], (z * 4 + q, g))

    def ma_copy(k):
        q = lax.rem(g + k, 8)
        return copy(m12.at[q], arecv.at[k - 1], ma_s.at[k - 1], ma_r.at[k - 1], (t, q))

    def mb_copy(k):
        q = lax.rem(v + k, 8)
        return copy(msg.at[q], r1.at[k - 1], mb_s.at[k - 1], mb_r.at[k - 1], (u * 8 + q, g))

    def mc_send(b):
        return copy(msg.at[8 + b], r2.at[u], mc_s.at[b], mc_r.at[u], (v * 4 + b, g))

    def mc_recv(k):
        return copy(msg.at[8], r2.at[k], mc_s.at[0], mc_r.at[k], (k * 8 + lax.div(t, 4), g))

    barrier = pltpu.get_barrier_semaphore()
    others = [ring_dev(0, step(X, 3 - 2 * xl))]
    others += [(z * 4 + step(s, k), g) for k in (1, 2, 3)]
    others += [(t, lax.rem(g + k, 8)) for k in range(1, 8)]
    others += [(lax.rem(z + k, 8) * 4 + s, g) for k in range(1, 8)]
    others += [((z + 1 - 2 * lax.rem(z, 2)) * 4 + step(s, k), g) for k in (1, 2, 3)]
    for dev in others:
        pl.semaphore_signal(barrier, inc=1, device_id=dev, device_id_type=MESH)
    for k in range(4):
        source = k * 8 + lax.div(t, 4)

        @pl.when(source != t)
        def _():
            pl.semaphore_signal(barrier, inc=1, device_id=(source, g), device_id_type=MESH)

    def columns(ref, base):
        return ref.at[:, pl.ds(pl.multiple_of(base, T), T)]

    loads = [
        (core_z, cz), (columns(core_y, v * T), cy.at[0]), (columns(core_y, (v + 1 - 2 * c) * T), cy.at[1]),
        (z_first, tz1), (z_second, tz2), (columns(y_first, v * T), ty1), (columns(y_third, v * T), ty3),
        (columns(x_second, u * T), tx2), (columns(x_third, u * T), tx3), (columns(core_x, u * T), cx),
    ]
    loads = [pltpu.make_async_copy(a, b, in_s.at[k]) for k, (a, b) in enumerate(loads)]
    for load in loads:
        load.start()

    def start_own(ch, _):
        own_copy(ch).start()
        return 0

    lax.fori_loop(0, NCH, start_own, 0)

    @pl.when(lax.div(t, 4) == v)
    def _():
        pl.semaphore_wait(barrier, len(others) + 3)

    @pl.when(lax.div(t, 4) != v)
    def _():
        pl.semaphore_wait(barrier, len(others) + 4)

    def start_par(ch, _):
        par_copy(ch).start()
        return 0

    lax.fori_loop(0, NCH, start_par, 0)
    for load in loads:
        load.wait()

    def r_of(row):
        h = jnp.where(row >= 48, 1, 0)
        rest = row - 48 * h
        e = rest & 15
        return 24 * (((e >> 2) & 1) * 4 + (e & 3)) + 12 * (e >> 3) + 6 * c + 3 * h + (rest >> 4)

    def eights(n):
        return lambda row: jnp.where((row & 7) < n, n * (row >> 3) + (row & 7), -1)

    eye = pick(T, T, lambda row: row)
    gap = jnp.zeros((32, T), BF16)
    czt[...] = nn(pick(96, S, r_of), cz[...]).astype(BF16)
    for o in range(2):
        low, high = cy[o, 0:128], cy[o, 128:192]
        wy[0, o * T : o * T + T, :] = nt(eye, jnp.concatenate([low, high, gap, gap], axis=0)).astype(BF16)
        wy[1, o * T : o * T + T, :] = nt(eye, jnp.concatenate([low, gap, gap, high], axis=0)).astype(BF16)
    zp[...] = nt(eye, jnp.concatenate([tz1[...], gap, tz2[...], gap], axis=0)).astype(BF16)
    y1[...] = nt(eye, jnp.concatenate([ty1[...], gap], axis=0))
    x2[...] = nt(eye, jnp.concatenate([tx2[...], gap], axis=0))
    turned = tx3[...].astype(F32)
    for n in range(T // MODE):
        x3[n, :, 0:MODE] = turned[:, n * MODE : n * MODE + MODE]
    cxp[...] = nn(pick(256, S, eights(6)), cx[...]).astype(BF16)
    g2[...] = jnp.zeros_like(g2)
    g3[...] = jnp.zeros_like(g3)

    def contract_z(ch):
        own_copy(ch).wait()
        par_copy(ch).wait_recv()
        for a in range(CH):
            both = jnp.concatenate([own[ch, a], par[ch, a]], axis=0)
            w = nt(czt[...], both).astype(BF16)
            for h in range(2):
                for i in range(PARTS):
                    at = (h * PARTS + i) * 16
                    wt[h, i, ch, a * 16 : a * 16 + 16, :] = w[at : at + 16]

    def contract_y(n):
        i, ch, d = lax.div(n, NCH), lax.rem(n, NCH), lax.rem(n, 2)
        for b in range(4):
            top = nn(wt[0, i, ch, b * 128 : b * 128 + 128, :], wy[0])
            bot = nn(wt[1, i, ch, b * 128 : b * 128 + 128, :], wy[1])
            rest = top[:, 128:] + bot[:, 128:]
            for a in range(8):
                at, lo = (b * 8 + a) * 48, a * 16
                us[at : at + 16, :] = top[lo : lo + 16, 0:128]
                us[at + 16 : at + 32, :] = bot[lo : lo + 16, 0:128]
                us[at + 32 : at + 48, :] = rest[lo : lo + 16]
        for e in range(16):
            q = (1 - d) * e + d * ((e % 4) * 4 + e // 4)
            for kind in range(3):
                block = us[pl.ds(kind * 16 + e, CH, stride=48), :]
                send[n, q, kind * CH : kind * CH + CH, :] = block.astype(BF16)
        for w in range(2):
            mid_copy(n, w).start()
        for w in range(2):
            dir_copy(n, w).start()

    def modes(n):
        ch, off = lax.div(n, 2), lax.rem(n, 2) * MODE
        rows = x2[pl.ds(pl.multiple_of(n * MODE, MODE), MODE), :]
        total = g2[...]
        factors = []
        for a in range(MODE):
            m = nn(own[ch, off + a], zp[...])
            g1[pl.ds(n * MODE + a, 1), :] = jnp.sum(m[:, 0:128] * y1[...], axis=0, keepdims=True)
            total = total + m[:, 128:] * rows[a : a + 1]
            factors.append((ty3[...].astype(F32) * x3[n, :, a : a + 1]).astype(BF16))
        g2[...] = total
        block = own[ch, pl.ds(off, MODE)].reshape(MODE * T, T)
        g3[...] += nn(jnp.concatenate(factors, axis=1), block)

    def forward(n):
        p = place(lax.rem(n, 2))
        for w in range(2):
            mid_copy(n, w).wait_recv()
            base = step(p, 1 + 2 * w) * 4 + 2 * w
            for h in range(2):
                mine = send[n, base + h].astype(F32)
                send[n, base + h] = (mine + mid[n, w, h].astype(F32)).astype(BF16)
            com_copy(n, w).start()

    def finish(n):
        p = place(lax.rem(n, 2))
        for w in range(2):
            dir_copy(n, w).wait_recv()
            com_copy(n, w).wait_recv()
        for b in range(4):
            tot = send[n, p * 4 + b].astype(F32) + ring[n, 0, b].astype(F32) + ring[n, 1, b].astype(F32)
            send[n, p * 4 + b] = tot.astype(BF16)
        for k in (1, 2, 3):
            sec_copy(n, k).start()

    def collect(n):
        i, ch, d = lax.div(n, NCH), lax.rem(n, NCH), lax.rem(n, 2)
        for k in (1, 2, 3):
            sec_copy(n, k).wait_recv()
        tot = send[n, place(d) * 4 + place(1 - d)].astype(F32)
        for k in range(3):
            tot = tot + second[n, k].astype(F32)
        tot = tot.astype(BF16)
        for kind in range(3):
            gath[i, kind, pl.ds(pl.multiple_of(ch * CH, CH), CH), :] = tot[kind * CH : kind * CH + CH]

    def contract_x(i):
        for kind in range(3):
            piece = nn(cxp[...], gath[i, kind])
            hbuf[i, :, kind * 32 : kind * 32 + 32, :] = piece.astype(BF16).reshape(8, 32, T)
        if i == 1:
            piece = nn(pick(256, K, eights(3)), g3[...].astype(BF16))
            hbuf[i, :, 96:128, :] = piece.astype(BF16).reshape(8, 32, T)
        for k in (4, 3, 5, 2, 6, 1, 7):
            z_copy(i, k).start()

    def finish_z(i):
        for k in range(1, 8):
            z_copy(i, k).wait_recv()
        for kind in range(4 if i == 1 else 3):
            at = kind * 32
            tot = hbuf[i, z, at : at + 32, :].astype(F32)
            for k in range(7):
                tot = tot + zrecv[i, k, at : at + 32, :].astype(F32)
            fbuf[i, :, kind] = tot.reshape(4, 8, T)
        for k in (1, 2, 3):
            f_copy(i, k).start()

    def modes_a():
        high = lax.Precision.HIGHEST
        one = nn(pick(T, T, lambda q: 16 * ((q >> 1) & 7) + 2 * (q >> 4) + (q & 1), F32), g1[...], high)
        two = nn(pick(T, T, lambda q: 32 * ((q >> 2) & 3) + 4 * (q >> 4) + (q & 3), F32), g2[...], high)
        m12[:, 0:16, :] = one.reshape(8, 16, T)
        m12[:, 16:32, :] = two.reshape(8, 16, T)
        for k in range(1, 8):
            ma_copy(k).start()

    def modes_b():
        total = m12[g]
        for k in range(1, 8):
            ma_copy(k).wait_recv()
            total = total + arecv[k - 1]

        def source_row(q):
            i = q & 7
            low = jnp.where(i < 2, 2 * (q >> 3) + i, -1)
            return jnp.where(q < 64, low, jnp.where(i < 4, 16 + 4 * ((q - 64) >> 3) + i, -1))

        msg[...] = nn(pick(96, 32, source_row, F32), total, lax.Precision.HIGHEST).reshape(12, 8, T)
        for k in range(1, 8):
            mb_copy(k).start()
        for b in range(4):

            @pl.when(v * 4 + b != t)
            def _():
                mc_send(b).start()

            @pl.when(v * 4 + b == t)
            def _():
                r2[u] = msg[8 + b]

    def turn(n, _):
        @pl.when(n < NCH)
        def _():
            contract_z(n)

        @pl.when(n < UNITS)
        def _():
            contract_y(n)

        @pl.when((n >= FORWARD) & (n < UNITS + FORWARD))
        def _():
            forward(n - FORWARD)

        @pl.when(n < T // MODE)
        def _():
            modes(n)

        @pl.when((n >= FINISH) & (n < UNITS + FINISH))
        def _():
            finish(n - FINISH)

        @pl.when((n >= COLLECT) & (n < UNITS + COLLECT))
        def _():
            collect(n - COLLECT)

        for i in range(PARTS):
            last = NCH * i + NCH - 1 + COLLECT

            @pl.when(n == last)
            def _():
                contract_x(i)

            @pl.when(n == last + ZLAG)
            def _():
                finish_z(i)

        @pl.when(n == MODE_A)
        def _():
            modes_a()

        @pl.when(n == MODE_B)
        def _():
            modes_b()

        return 0

    lax.fori_loop(0, UNITS + COLLECT + ZLAG, turn, 0)

    first = msg[v]
    for k in range(1, 8):
        mb_copy(k).wait_recv()
        first = first + r1[k - 1]
    out[37] = first
    for k in range(4):

        @pl.when(k * 8 + lax.div(t, 4) != t)
        def _():
            mc_recv(k).wait_recv()

    out[38] = r2[0] + r2[1] + r2[2] + r2[3]
    third = fbuf[1, s, 3]
    for i in range(PARTS):
        for kind in range(3):
            out[s * 9 + kind * 3 + i] = fbuf[i, s, kind]
        for k in (1, 2, 3):
            f_copy(i, k).wait_recv()
            for kind in range(3):
                out[step(s, 4 - k) * 9 + kind * 3 + i] = frecv[i, k - 1, kind]
            if i == 1:
                third = third + frecv[1, k - 1, 3]
    out[36] = third

    def drain(n, _):
        for w in range(2):
            mid_copy(n, w).wait_send()
            dir_copy(n, w).wait_send()
            com_copy(n, w).wait_send()
        for k in (1, 2, 3):
            sec_copy(n, k).wait_send()
        return 0

    lax.fori_loop(0, UNITS, drain, 0)
    for ch in range(NCH):
        par_copy(ch).wait_send()
    for i in range(PARTS):
        for k in range(1, 8):
            z_copy(i, k).wait_send()
        for k in (1, 2, 3):
            f_copy(i, k).wait_send()
    for k in range(1, 8):
        ma_copy(k).wait_send()
        mb_copy(k).wait_send()
    for b in range(4):

        @pl.when(v * 4 + b != t)
        def _():
            mc_send(b).wait_send()


def outputs_kernel(x, one, two, three, core):
    one[...] = x[37 * 8 : 37 * 8 + 2, 0:K]
    two[...] = x[38 * 8 : 38 * 8 + 4, 0:K]
    three[...] = x[36 * 8 : 36 * 8 + 3, :]
    for p in range(6):
        rows = x[pl.ds(p, 36, stride=8), :]
        for q in range(4):
            core[p, 6 * q : 6 * q + 6, 0:128] = rows[9 * q : 9 * q + 6]
            core[p, 6 * q : 6 * q + 3, 128:192] = rows[9 * q + 6 : 9 * q + 9, 0:64]
            core[p, 6 * q + 3 : 6 * q + 6, 128:192] = rows[9 * q + 6 : 9 * q + 9, 64:128]


def shards(field, *small):
    vm, hbm = pl.BlockSpec(memory_space=pltpu.VMEM), pl.BlockSpec(memory_space=pl.ANY)
    dma, mem = pltpu.SemaphoreType.DMA, pltpu.VMEM
    unit = [dma((UNITS, 2))] * 6 + [dma((UNITS, 3))] * 2
    raw = pl.pallas_call(
        main_kernel,
        out_shape=jax.ShapeDtypeStruct((39, 8, 128), F32),
        in_specs=[hbm] * 10,
        out_specs=vm,
        scratch_shapes=[
            mem((NCH, CH, T, T), BF16),
            mem((NCH, CH, T, T), BF16),
            mem((2, PARTS, NCH, CH * 16, 256), BF16),
            mem((CH * 48, 128), F32),
            mem((UNITS, 16, ROWS, 128), BF16),
            mem((UNITS, 2, 2, ROWS, 128), BF16),
            mem((UNITS, 2, 4, ROWS, 128), BF16),
            mem((UNITS, 3, ROWS, 128), BF16),
            mem((PARTS, 3, T, 128), BF16),
            mem((PARTS, 8, 128, 128), BF16),
            mem((PARTS, 7, 128, 128), BF16),
            mem((PARTS, 4, 4, 8, 128), F32),
            mem((PARTS, 3, 4, 8, 128), F32),
            mem((S, T), BF16), mem((2, S, T), BF16), mem((S, T), BF16),
            mem((K, T), BF16), mem((K, T), BF16), mem((K, T), BF16), mem((K, T), BF16),
            mem((K, T), BF16), mem((K, T), BF16),
            mem((K, T), BF16),
            mem((256, T), BF16),
            mem((2, 2 * T, 256), BF16),
            mem((T, 256), BF16),
            mem((T, 128), F32), mem((T, 128), F32),
            mem((T // MODE, K, 128), F32),
            mem((T, 128), F32), mem((T, 128), F32), mem((K, T), F32),
            mem((8, 32, 128), F32), mem((7, 32, 128), F32),
            mem((12, 8, 128), F32), mem((7, 8, 128), F32), mem((4, 8, 128), F32),
            dma((10,)), dma((NCH,)), dma((NCH,)), dma((NCH,)),
            *unit,
            dma((PARTS, 7)), dma((PARTS, 7)), dma((PARTS, 3)), dma((PARTS, 3)),
            dma((7,)), dma((7,)), dma((7,)), dma((7,)), dma((4,)), dma((4,)),
        ],
        compiler_params=pltpu.CompilerParams(
            collective_id=0, has_side_effects=True, vmem_limit_bytes=56 * 1024 * 1024
        ),
    )(field, *[x.T for x in small])
    one, two, three, core = pl.pallas_call(
        outputs_kernel,
        out_shape=(
            jax.ShapeDtypeStruct((2, K), F32),
            jax.ShapeDtypeStruct((4, K), F32),
            jax.ShapeDtypeStruct((3, T), F32),
            jax.ShapeDtypeStruct((6, 24, S), F32),
        ),
        in_specs=[vm],
        out_specs=(vm, vm, vm, vm),
    )(raw.reshape(39 * 8, 128))
    return (one, two, three, core.transpose(0, 2, 1))


def solution(mesh):
    return jax.shard_map(
        shards,
        mesh=mesh,
        in_specs=(
            P("xy", None, None, "gz"),
            P(), P(), P("gz", None), P(), P(), P(), P(), P("gz", None), P("gz", None),
        ),
        out_specs=(
            P(("xy", "gz"), None),
            P(("xy", "gz"), None),
            P("xy", "gz"),
            P("xy", None, "gz"),
        ),
        check_vma=False,
    )
```

```python
import jax
import jax.numpy as jnp
from jax import lax
from jax.experimental import pallas as pl
from jax.experimental.pallas import tpu as pltpu
from jax.sharding import PartitionSpec as P

MESH = pl.DeviceIdType.MESH
F32, BF16, I32 = jnp.float32, jnp.bfloat16, jnp.int32
K = 96
S = 192
T = 128
CH = 32
NCH = T // CH
PARTS = 3
UNITS = PARTS * NCH
ROWS = 3 * CH
MODE = 16
DIRECT, FORWARD, FINISH, COLLECT, ZLAG = 1, 2, 5, 8, 6
MODE_0, MODE_A, MODE_B = 4, 12, 16


def nn(a, b, precision=None):
    return lax.dot_general(a, b, (((1,), (0,)), ((), ())), preferred_element_type=F32, precision=precision)


def nt(a, b):
    return lax.dot_general(a, b, (((1,), (1,)), ((), ())), preferred_element_type=F32)


def pick(rows, columns, column_of, dtype=BF16):
    r = lax.broadcasted_iota(I32, (rows, columns), 0)
    return jnp.where(lax.broadcasted_iota(I32, (rows, columns), 1) == column_of(r), 1.0, 0.0).astype(dtype)


def main_kernel(
    field, core_x, core_y, core_z, x_second, x_third, y_first, y_third, z_first, z_second,
    out,
    own, par, wt, us, send, mid, ring, second, gath, hbuf, zrecv, fbuf, frecv,
    cx, cy, cz, tx2, tx3, ty1, ty3, tz1, tz2,
    czt, cxp, wy, zp, y1, x2, x3, g1, g2, g3, m12, arecv, msg, r1, r2,
    in_s, own_sem, par_s, par_r, mid_s, mid_r, dir_s, dir_r, com_s, com_r, sec_s, sec_r, z_s, z_r, f_s, f_r,
    ma_s, ma_r, mb_s, mb_r, mc_s, mc_r,
):
    t, g = lax.axis_index("xy"), lax.axis_index("gz")
    z, s = lax.div(t, 4), lax.rem(t, 4)
    xh, c = lax.div(s, 2), lax.rem(s, 2)
    xl, y = lax.div(g, 4), lax.rem(g, 4)
    X = xh * 2 + xl
    u, v = lax.div(t, 8), lax.rem(t, 8)
    mate = t + 1 - 2 * c

    def ring_dev(d, q):
        tt = t + (1 - d) * 2 * (lax.div(q, 2) - xh)
        gg = g + (1 - d) * 4 * (lax.rem(q, 2) - xl) + d * (q - y)
        return (tt, gg)

    def place(d):
        return (1 - d) * X + d * y

    def step(p, k):
        return lax.rem(p + k, 4)

    def copy(src, dst, ss, rs, dev):
        return pltpu.make_async_remote_copy(
            src_ref=src, dst_ref=dst, send_sem=ss, recv_sem=rs, device_id=dev, device_id_type=MESH
        )

    def own_copy(ch):
        return pltpu.make_async_copy(field.at[0, pl.ds(ch * CH, CH)], own.at[ch], own_sem.at[ch])

    def par_copy(ch):
        return copy(own.at[ch], par.at[ch], par_s.at[ch], par_r.at[ch], (mate, g))

    def mid_copy(n, w):
        d = lax.rem(n, 2)
        p = place(d)
        src = send.at[n, pl.ds(step(p, 2) * 4 + 2 * w, 2)]
        return copy(src, mid.at[n, w], mid_s.at[n, w], mid_r.at[n, w], ring_dev(d, step(p, 1 + 2 * w)))

    def part(n, w, h):
        p = place(lax.rem(n, 2))
        return send.at[n, pl.ds(step(p, 1 + 2 * w) * 4 + 2 * h, 2)]

    def dir_copy(n, w):
        d = lax.rem(n, 2)
        dst = ring.at[n, w, pl.ds(2 * (1 - w), 2)]
        return copy(part(n, w, 1 - w), dst, dir_s.at[n, w], dir_r.at[n, w], ring_dev(d, step(place(d), 1 + 2 * w)))

    def com_copy(n, w):
        d = lax.rem(n, 2)
        dst = ring.at[n, w, pl.ds(2 * w, 2)]
        return copy(part(n, w, w), dst, com_s.at[n, w], com_r.at[n, w], ring_dev(d, step(place(d), 1 + 2 * w)))

    def sec_copy(n, k):
        d = lax.rem(n, 2)
        q = step(place(1 - d), k)
        src = send.at[n, place(d) * 4 + q]
        return copy(src, second.at[n, k - 1], sec_s.at[n, k - 1], sec_r.at[n, k - 1], ring_dev(1 - d, q))

    def z_copy(i, k):
        zz = lax.rem(z + k, 8)
        size = 128 if i == 1 else 96
        src, dst = hbuf.at[i, zz, pl.ds(0, size)], zrecv.at[i, k - 1, pl.ds(0, size)]
        return copy(src, dst, z_s.at[i, k - 1], z_r.at[i, k - 1], (zz * 4 + s, g))

    def f_copy(i, k):
        q = step(s, k)
        size = 4 if i == 1 else 3
        src, dst = fbuf.at[i, q, pl.ds(0, size)], frecv.at[i, k - 1, pl.ds(0, size)]
        return copy(src, dst, f_s.at[i, k - 1], f_r.at[i, k - 1], (z * 4 + q, g))

    def ma_copy(k):
        q = lax.rem(g + k, 8)
        return copy(m12.at[q], arecv.at[k - 1], ma_s.at[k - 1], ma_r.at[k - 1], (t, q))

    def mb_copy(k):
        q = lax.rem(v + k, 8)
        return copy(msg.at[q], r1.at[k - 1], mb_s.at[k - 1], mb_r.at[k - 1], (u * 8 + q, g))

    def mc_send(b):
        return copy(msg.at[8 + b], r2.at[u], mc_s.at[b], mc_r.at[u], (v * 4 + b, g))

    def mc_recv(k):
        return copy(msg.at[8], r2.at[k], mc_s.at[0], mc_r.at[k], (k * 8 + lax.div(t, 4), g))

    barrier = pltpu.get_barrier_semaphore()
    others = [ring_dev(0, step(X, 3 - 2 * xl))]
    others += [(z * 4 + step(s, k), g) for k in (1, 2, 3)]
    others += [(t, lax.rem(g + k, 8)) for k in range(1, 8)]
    others += [(lax.rem(z + k, 8) * 4 + s, g) for k in range(1, 8)]
    others += [((z + 1 - 2 * lax.rem(z, 2)) * 4 + step(s, k), g) for k in (1, 2, 3)]
    for dev in others:
        pl.semaphore_signal(barrier, inc=1, device_id=dev, device_id_type=MESH)
    for k in range(4):
        source = k * 8 + lax.div(t, 4)

        @pl.when(source != t)
        def _():
            pl.semaphore_signal(barrier, inc=1, device_id=(source, g), device_id_type=MESH)

    def columns(ref, base):
        return ref.at[:, pl.ds(pl.multiple_of(base, T), T)]

    loads = [
        (core_z, cz), (columns(core_y, v * T), cy.at[0]), (columns(core_y, (v + 1 - 2 * c) * T), cy.at[1]),
        (z_first, tz1), (z_second, tz2), (columns(y_first, v * T), ty1), (columns(y_third, v * T), ty3),
        (columns(x_second, u * T), tx2), (columns(x_third, u * T), tx3), (columns(core_x, u * T), cx),
    ]
    loads = [pltpu.make_async_copy(a, b, in_s.at[k]) for k, (a, b) in enumerate(loads)]
    for load in loads:
        load.start()

    def start_own(ch, _):
        own_copy(ch).start()
        return 0

    lax.fori_loop(0, NCH, start_own, 0)

    @pl.when(lax.div(t, 4) == v)
    def _():
        pl.semaphore_wait(barrier, len(others) + 3)

    @pl.when(lax.div(t, 4) != v)
    def _():
        pl.semaphore_wait(barrier, len(others) + 4)

    own_copy(0).wait()
    par_copy(0).start()
    for load in loads:
        load.wait()

    def r_of(row):
        h = jnp.where(row >= 48, 1, 0)
        rest = row - 48 * h
        e = rest & 15
        return 24 * (((e >> 2) & 1) * 4 + (e & 3)) + 12 * (e >> 3) + 6 * c + 3 * h + (rest >> 4)

    def eights(n):
        return lambda row: jnp.where((row & 7) < n, n * (row >> 3) + (row & 7), -1)

    eye = pick(T, T, lambda row: row)
    gap = jnp.zeros((32, T), BF16)
    czt[...] = nn(pick(96, S, r_of), cz[...]).astype(BF16)
    for o in range(2):
        low, high = cy[o, 0:128], cy[o, 128:192]
        wy[0, o * T : o * T + T, :] = nt(eye, jnp.concatenate([low, high, gap, gap], axis=0)).astype(BF16)
        wy[1, o * T : o * T + T, :] = nt(eye, jnp.concatenate([low, gap, gap, high], axis=0)).astype(BF16)
    zp[...] = nt(eye, jnp.concatenate([tz1[...], gap, tz2[...], gap], axis=0)).astype(BF16)
    y1[...] = nt(eye, jnp.concatenate([ty1[...], gap], axis=0))
    x2[...] = nt(eye, jnp.concatenate([tx2[...], gap], axis=0))
    turned = tx3[...].astype(F32)
    for n in range(T // MODE):
        x3[n, :, 0:MODE] = turned[:, n * MODE : n * MODE + MODE]
    cxp[...] = nn(pick(256, S, eights(6)), cx[...]).astype(BF16)
    g2[...] = jnp.zeros_like(g2)
    g3[...] = jnp.zeros_like(g3)

    def start_par(ch):
        own_copy(ch).wait()
        par_copy(ch).start()

    start_par(1)

    def contract_z(ch):
        par_copy(ch).wait_recv()

        @pl.when(ch < NCH - 2)
        def _():
            start_par(ch + 2)

        for a in range(CH):
            both = jnp.concatenate([own[ch, a], par[ch, a]], axis=0)
            w = nt(czt[...], both).astype(BF16)
            for h in range(2):
                for i in range(PARTS):
                    at = (h * PARTS + i) * 16
                    wt[h, i, ch, a * 16 : a * 16 + 16, :] = w[at : at + 16]

    def contract_y(n):
        i, ch, d = lax.div(n, NCH), lax.rem(n, NCH), lax.rem(n, 2)
        for b in range(4):
            top = nn(wt[0, i, ch, b * 128 : b * 128 + 128, :], wy[0])
            bot = nn(wt[1, i, ch, b * 128 : b * 128 + 128, :], wy[1])
            rest = top[:, 128:] + bot[:, 128:]
            for a in range(8):
                at, lo = (b * 8 + a) * 48, a * 16
                us[at : at + 16, :] = top[lo : lo + 16, 0:128]
                us[at + 16 : at + 32, :] = bot[lo : lo + 16, 0:128]
                us[at + 32 : at + 48, :] = rest[lo : lo + 16]
        for e in range(16):
            q = (1 - d) * e + d * ((e % 4) * 4 + e // 4)
            for kind in range(3):
                block = us[pl.ds(kind * 16 + e, CH, stride=48), :]
                send[n, q, kind * CH : kind * CH + CH, :] = block.astype(BF16)
        for w in range(2):
            mid_copy(n, w).start()

    def modes(n):
        ch, off = lax.div(n, 2), lax.rem(n, 2) * MODE
        rows = x2[pl.ds(pl.multiple_of(n * MODE, MODE), MODE), :]
        total = g2[...]
        factors = []
        for a in range(MODE):
            m = nn(own[ch, off + a], zp[...])
            g1[pl.ds(n * MODE + a, 1), :] = jnp.sum(m[:, 0:128] * y1[...], axis=0, keepdims=True)
            total = total + m[:, 128:] * rows[a : a + 1]
            factors.append((ty3[...].astype(F32) * x3[n, :, a : a + 1]).astype(BF16))
        g2[...] = total
        block = own[ch, pl.ds(off, MODE)].reshape(MODE * T, T)
        g3[...] += nn(jnp.concatenate(factors, axis=1), block)

    def forward(n):
        p = place(lax.rem(n, 2))
        for w in range(2):
            mid_copy(n, w).wait_recv()
            base = step(p, 1 + 2 * w) * 4 + 2 * w
            for h in range(2):
                mine = send[n, base + h].astype(F32)
                send[n, base + h] = (mine + mid[n, w, h].astype(F32)).astype(BF16)
            com_copy(n, w).start()

    def finish(n):
        p = place(lax.rem(n, 2))
        for w in range(2):
            dir_copy(n, w).wait_recv()
            com_copy(n, w).wait_recv()
        for b in range(4):
            tot = send[n, p * 4 + b].astype(F32) + ring[n, 0, b].astype(F32) + ring[n, 1, b].astype(F32)
            send[n, p * 4 + b] = tot.astype(BF16)
        for k in (1, 2, 3):
            sec_copy(n, k).start()

    def collect(n):
        i, ch, d = lax.div(n, NCH), lax.rem(n, NCH), lax.rem(n, 2)
        for k in (1, 2, 3):
            sec_copy(n, k).wait_recv()
        tot = send[n, place(d) * 4 + place(1 - d)].astype(F32)
        for k in range(3):
            tot = tot + second[n, k].astype(F32)
        tot = tot.astype(BF16)
        for kind in range(3):
            gath[i, kind, pl.ds(pl.multiple_of(ch * CH, CH), CH), :] = tot[kind * CH : kind * CH + CH]

    def contract_x(i):
        for kind in range(3):
            piece = nn(cxp[...], gath[i, kind])
            hbuf[i, :, kind * 32 : kind * 32 + 32, :] = piece.astype(BF16).reshape(8, 32, T)
        if i == 1:
            piece = nn(pick(256, K, eights(3)), g3[...].astype(BF16))
            hbuf[i, :, 96:128, :] = piece.astype(BF16).reshape(8, 32, T)
        for k in (4, 3, 5, 2, 6, 1, 7):
            z_copy(i, k).start()

    def finish_z(i):
        for k in range(1, 8):
            z_copy(i, k).wait_recv()
        for kind in range(4 if i == 1 else 3):
            at = kind * 32
            tot = hbuf[i, z, at : at + 32, :].astype(F32)
            for k in range(7):
                tot = tot + zrecv[i, k, at : at + 32, :].astype(F32)
            fbuf[i, :, kind] = tot.reshape(4, 8, T)
        for k in (1, 2, 3):
            f_copy(i, k).start()

    def modes_a():
        high = lax.Precision.HIGHEST
        one = nn(pick(T, T, lambda q: 16 * ((q >> 1) & 7) + 2 * (q >> 4) + (q & 1), F32), g1[...], high)
        two = nn(pick(T, T, lambda q: 32 * ((q >> 2) & 3) + 4 * (q >> 4) + (q & 3), F32), g2[...], high)
        m12[:, 0:16, :] = one.reshape(8, 16, T)
        m12[:, 16:32, :] = two.reshape(8, 16, T)
        for k in range(1, 8):
            ma_copy(k).start()

    def modes_b():
        total = m12[g]
        for k in range(1, 8):
            ma_copy(k).wait_recv()
            total = total + arecv[k - 1]

        def source_row(q):
            i = q & 7
            low = jnp.where(i < 2, 2 * (q >> 3) + i, -1)
            return jnp.where(q < 64, low, jnp.where(i < 4, 16 + 4 * ((q - 64) >> 3) + i, -1))

        msg[...] = nn(pick(96, 32, source_row, F32), total, lax.Precision.HIGHEST).reshape(12, 8, T)
        for k in range(1, 8):
            mb_copy(k).start()
        for b in range(4):

            @pl.when(v * 4 + b != t)
            def _():
                mc_send(b).start()

            @pl.when(v * 4 + b == t)
            def _():
                r2[u] = msg[8 + b]

    def turn(n, _):
        @pl.when(n < NCH)
        def _():
            contract_z(n)

        @pl.when(n < UNITS)
        def _():
            contract_y(n)

        @pl.when((n >= DIRECT) & (n < UNITS + DIRECT))
        def _():
            for w in range(2):
                dir_copy(n - DIRECT, w).start()

        @pl.when((n >= FORWARD) & (n < UNITS + FORWARD))
        def _():
            forward(n - FORWARD)

        @pl.when((n >= MODE_0) & (n < MODE_0 + T // MODE))
        def _():
            modes(n - MODE_0)

        @pl.when((n >= FINISH) & (n < UNITS + FINISH))
        def _():
            finish(n - FINISH)

        @pl.when((n >= COLLECT) & (n < UNITS + COLLECT))
        def _():
            collect(n - COLLECT)

        for i in range(PARTS):
            last = NCH * i + NCH - 1 + COLLECT

            @pl.when(n == last)
            def _():
                contract_x(i)

            @pl.when(n == last + ZLAG)
            def _():
                finish_z(i)

        @pl.when(n == MODE_A)
        def _():
            modes_a()

        @pl.when(n == MODE_B)
        def _():
            modes_b()

        return 0

    lax.fori_loop(0, UNITS + COLLECT + ZLAG, turn, 0)

    first = msg[v]
    for k in range(1, 8):
        mb_copy(k).wait_recv()
        first = first + r1[k - 1]
    out[37] = first
    for k in range(4):

        @pl.when(k * 8 + lax.div(t, 4) != t)
        def _():
            mc_recv(k).wait_recv()

    out[38] = r2[0] + r2[1] + r2[2] + r2[3]
    third = fbuf[1, s, 3]
    for i in range(PARTS):
        for kind in range(3):
            out[s * 9 + kind * 3 + i] = fbuf[i, s, kind]
        for k in (1, 2, 3):
            f_copy(i, k).wait_recv()
            for kind in range(3):
                out[step(s, 4 - k) * 9 + kind * 3 + i] = frecv[i, k - 1, kind]
            if i == 1:
                third = third + frecv[1, k - 1, 3]
    out[36] = third

    def drain(n, _):
        for w in range(2):
            mid_copy(n, w).wait_send()
            dir_copy(n, w).wait_send()
            com_copy(n, w).wait_send()
        for k in (1, 2, 3):
            sec_copy(n, k).wait_send()
        return 0

    lax.fori_loop(0, UNITS, drain, 0)
    for ch in range(NCH):
        par_copy(ch).wait_send()
    for i in range(PARTS):
        for k in range(1, 8):
            z_copy(i, k).wait_send()
        for k in (1, 2, 3):
            f_copy(i, k).wait_send()
    for k in range(1, 8):
        ma_copy(k).wait_send()
        mb_copy(k).wait_send()
    for b in range(4):

        @pl.when(v * 4 + b != t)
        def _():
            mc_send(b).wait_send()


def outputs_kernel(x, one, two, three, core):
    one[...] = x[37 * 8 : 37 * 8 + 2, 0:K]
    two[...] = x[38 * 8 : 38 * 8 + 4, 0:K]
    three[...] = x[36 * 8 : 36 * 8 + 3, :]
    for p in range(6):
        rows = x[pl.ds(p, 36, stride=8), :]
        for q in range(4):
            core[p, 6 * q : 6 * q + 6, 0:128] = rows[9 * q : 9 * q + 6]
            core[p, 6 * q : 6 * q + 3, 128:192] = rows[9 * q + 6 : 9 * q + 9, 0:64]
            core[p, 6 * q + 3 : 6 * q + 6, 128:192] = rows[9 * q + 6 : 9 * q + 9, 64:128]


def shards(field, *small):
    vm, hbm = pl.BlockSpec(memory_space=pltpu.VMEM), pl.BlockSpec(memory_space=pl.ANY)
    dma, mem = pltpu.SemaphoreType.DMA, pltpu.VMEM
    unit = [dma((UNITS, 2))] * 6 + [dma((UNITS, 3))] * 2
    raw = pl.pallas_call(
        main_kernel,
        out_shape=jax.ShapeDtypeStruct((39, 8, 128), F32),
        in_specs=[hbm] * 10,
        out_specs=vm,
        scratch_shapes=[
            mem((NCH, CH, T, T), BF16),
            mem((NCH, CH, T, T), BF16),
            mem((2, PARTS, NCH, CH * 16, 256), BF16),
            mem((CH * 48, 128), F32),
            mem((UNITS, 16, ROWS, 128), BF16),
            mem((UNITS, 2, 2, ROWS, 128), BF16),
            mem((UNITS, 2, 4, ROWS, 128), BF16),
            mem((UNITS, 3, ROWS, 128), BF16),
            mem((PARTS, 3, T, 128), BF16),
            mem((PARTS, 8, 128, 128), BF16),
            mem((PARTS, 7, 128, 128), BF16),
            mem((PARTS, 4, 4, 8, 128), F32),
            mem((PARTS, 3, 4, 8, 128), F32),
            mem((S, T), BF16), mem((2, S, T), BF16), mem((S, T), BF16),
            mem((K, T), BF16), mem((K, T), BF16), mem((K, T), BF16), mem((K, T), BF16),
            mem((K, T), BF16), mem((K, T), BF16),
            mem((K, T), BF16),
            mem((256, T), BF16),
            mem((2, 2 * T, 256), BF16),
            mem((T, 256), BF16),
            mem((T, 128), F32), mem((T, 128), F32),
            mem((T // MODE, K, 128), F32),
            mem((T, 128), F32), mem((T, 128), F32), mem((K, T), F32),
            mem((8, 32, 128), F32), mem((7, 32, 128), F32),
            mem((12, 8, 128), F32), mem((7, 8, 128), F32), mem((4, 8, 128), F32),
            dma((10,)), dma((NCH,)), dma((NCH,)), dma((NCH,)),
            *unit,
            dma((PARTS, 7)), dma((PARTS, 7)), dma((PARTS, 3)), dma((PARTS, 3)),
            dma((7,)), dma((7,)), dma((7,)), dma((7,)), dma((4,)), dma((4,)),
        ],
        compiler_params=pltpu.CompilerParams(
            collective_id=0, has_side_effects=True, vmem_limit_bytes=56 * 1024 * 1024
        ),
    )(field, *[x.T for x in small])
    one, two, three, core = pl.pallas_call(
        outputs_kernel,
        out_shape=(
            jax.ShapeDtypeStruct((2, K), F32),
            jax.ShapeDtypeStruct((4, K), F32),
            jax.ShapeDtypeStruct((3, T), F32),
            jax.ShapeDtypeStruct((6, 24, S), F32),
        ),
        in_specs=[vm],
        out_specs=(vm, vm, vm, vm),
    )(raw.reshape(39 * 8, 128))
    return (one, two, three, core.transpose(0, 2, 1))


def solution(mesh):
    return jax.shard_map(
        shards,
        mesh=mesh,
        in_specs=(
            P("xy", None, None, "gz"),
            P(), P(), P("gz", None), P(), P(), P(), P(), P("gz", None), P("gz", None),
        ),
        out_specs=(
            P(("xy", "gz"), None),
            P(("xy", "gz"), None),
            P("xy", "gz"),
            P("xy", None, "gz"),
        ),
        check_vma=False,
    )
```

```python
import jax
import jax.numpy as jnp
from jax import lax
from jax.experimental import pallas as pl
from jax.experimental.pallas import tpu as pltpu
from jax.sharding import PartitionSpec as P

MESH = pl.DeviceIdType.MESH
F32, BF16, I32 = jnp.float32, jnp.bfloat16, jnp.int32
K = 96
S = 192
T = 128
CH = 32
NCH = T // CH
PIECES = (((0, 0), (1, 0), (2, 0)), ((0, 1), (1, 1), (2, 1)), ((0, 2), (1, 2), (2, 2)))
THIRD = 1
PARTS = len(PIECES)
UNITS = PARTS * NCH
MOST = 3
ROWS = MOST * CH
MODE = 16
DIRECT, FORWARD, FINISH, COLLECT, ZLAG = 1, 2, 5, 8, 6
MODE_0, MODE_A, MODE_B = 4, 12, 16


def nn(a, b, precision=None):
    return lax.dot_general(a, b, (((1,), (0,)), ((), ())), preferred_element_type=F32, precision=precision)


def nt(a, b):
    return lax.dot_general(a, b, (((1,), (1,)), ((), ())), preferred_element_type=F32)


def pick(rows, columns, column_of, dtype=BF16):
    r = lax.broadcasted_iota(I32, (rows, columns), 0)
    return jnp.where(lax.broadcasted_iota(I32, (rows, columns), 1) == column_of(r), 1.0, 0.0).astype(dtype)


def main_kernel(
    field, core_x, core_y, core_z, x_second, x_third, y_first, y_third, z_first, z_second,
    out,
    own, par, wt, us, send, mid, ring, second, gath, hbuf, zrecv, fbuf, frecv,
    cx, cy, cz, tx2, tx3, ty1, ty3, tz1, tz2,
    czt, cxp, wy, zp, y1, x2, x3, g1, g2, g3, m12, arecv, msg, r1, r2,
    in_s, own_sem, par_s, par_r, mid_s, mid_r, dir_s, dir_r, com_s, com_r, sec_s, sec_r, z_s, z_r, f_s, f_r,
    ma_s, ma_r, mb_s, mb_r, mc_s, mc_r,
):
    t, g = lax.axis_index("xy"), lax.axis_index("gz")
    z, s = lax.div(t, 4), lax.rem(t, 4)
    xh, c = lax.div(s, 2), lax.rem(s, 2)
    xl, y = lax.div(g, 4), lax.rem(g, 4)
    X = xh * 2 + xl
    u, v = lax.div(t, 8), lax.rem(t, 8)
    mate = t + 1 - 2 * c

    def ring_dev(d, q):
        tt = t + (1 - d) * 2 * (lax.div(q, 2) - xh)
        gg = g + (1 - d) * 4 * (lax.rem(q, 2) - xl) + d * (q - y)
        return (tt, gg)

    def place(d):
        return (1 - d) * X + d * y

    def step(p, k):
        return lax.rem(p + k, 4)

    def copy(src, dst, ss, rs, dev):
        return pltpu.make_async_remote_copy(
            src_ref=src, dst_ref=dst, send_sem=ss, recv_sem=rs, device_id=dev, device_id_type=MESH
        )

    def own_copy(ch):
        return pltpu.make_async_copy(field.at[0, pl.ds(ch * CH, CH)], own.at[ch], own_sem.at[ch])

    def par_copy(ch):
        return copy(field.at[0, pl.ds(ch * CH, CH)], par.at[ch], par_s.at[ch], par_r.at[ch], (mate, g))

    def block(n, place_of, size):
        return send.at[n, place_of, pl.ds(0, size)]

    def mid_copy(n, w, size):
        d = lax.rem(n, 2)
        p = place(d)
        src, dst = block(n, pl.ds(step(p, 2) * 4 + 2 * w, 2), size), mid.at[n, pl.ds(2 * w, 2), pl.ds(0, size)]
        return copy(src, dst, mid_s.at[n, w], mid_r.at[n, w], ring_dev(d, step(p, 1 + 2 * w)))

    def opp_copy(n, size):
        d = lax.rem(n, 2)
        q = step(place(d), 2)
        src, dst = block(n, pl.ds(q * 4, 4), size), mid.at[n, pl.ds(0, 4), pl.ds(0, size)]
        return copy(src, dst, mid_s.at[n, 0], mid_r.at[n, 0], ring_dev(d, q))

    def near_copy(n, w, h, count, size, ss, rs):
        d = lax.rem(n, 2)
        q = step(place(d), 1 + 2 * w)
        src, dst = block(n, pl.ds(q * 4 + h, count), size), ring.at[n, w, pl.ds(h, count), pl.ds(0, size)]
        return copy(src, dst, ss.at[n, w], rs.at[n, w], ring_dev(d, q))

    def dir_copy(n, w, size):
        return near_copy(n, w, 2 * (1 - w), 2, size, dir_s, dir_r)

    def com_copy(n, w, size):
        return near_copy(n, w, 2 * w, 2, size, com_s, com_r)

    def all_copy(n, w, size):
        return near_copy(n, w, 0, 4, size, dir_s, dir_r)

    def sec_copy(n, k, size):
        d = lax.rem(n, 2)
        q = step(place(1 - d), k)
        src, dst = block(n, place(d) * 4 + q, size), second.at[n, k - 1, pl.ds(0, size)]
        return copy(src, dst, sec_s.at[n, k - 1], sec_r.at[n, k - 1], ring_dev(1 - d, q))

    def slabs(i):
        return len(PIECES[i]) + (i == THIRD)

    def lines(i):
        used = 24 * len(PIECES[i]) + (12 if i == THIRD else 0)
        return (used + 15) // 16 * 16

    def z_copy(i, k):
        zz = lax.rem(z + k, 8)
        size = lines(i)
        src, dst = hbuf.at[i, zz, pl.ds(0, size)], zrecv.at[i, k - 1, pl.ds(0, size)]
        return copy(src, dst, z_s.at[i, k - 1], z_r.at[i, k - 1], (zz * 4 + s, g))

    def f_copy(i, k):
        q = step(s, k)
        size = slabs(i)
        src, dst = fbuf.at[i, q, pl.ds(0, size)], frecv.at[i, k - 1, pl.ds(0, size)]
        return copy(src, dst, f_s.at[i, k - 1], f_r.at[i, k - 1], (z * 4 + q, g))

    def ma_copy(k):
        q = lax.rem(g + k, 8)
        return copy(m12.at[q], arecv.at[k - 1], ma_s.at[k - 1], ma_r.at[k - 1], (t, q))

    def mb_copy(k):
        q = lax.rem(v + k, 8)
        return copy(msg.at[q], r1.at[k - 1], mb_s.at[k - 1], mb_r.at[k - 1], (u * 8 + q, g))

    def mc_send(b):
        return copy(msg.at[8 + b], r2.at[u], mc_s.at[b], mc_r.at[u], (v * 4 + b, g))

    def mc_recv(k):
        return copy(msg.at[8], r2.at[k], mc_s.at[0], mc_r.at[k], (k * 8 + lax.div(t, 4), g))

    barrier = pltpu.get_barrier_semaphore()
    others = [ring_dev(0, step(X, 3 - 2 * xl))]
    others += [(z * 4 + step(s, k), g) for k in (1, 2, 3)]
    others += [(t, lax.rem(g + k, 8)) for k in range(1, 8)]
    others += [(lax.rem(z + k, 8) * 4 + s, g) for k in range(1, 8)]
    others += [((z + 1 - 2 * lax.rem(z, 2)) * 4 + step(s, k), g) for k in (1, 2, 3)]
    for dev in others:
        pl.semaphore_signal(barrier, inc=1, device_id=dev, device_id_type=MESH)
    for k in range(4):
        source = k * 8 + lax.div(t, 4)

        @pl.when(source != t)
        def _():
            pl.semaphore_signal(barrier, inc=1, device_id=(source, g), device_id_type=MESH)

    def columns(ref, base):
        return ref.at[:, pl.ds(pl.multiple_of(base, T), T)]

    loads = [
        (core_z, cz), (columns(core_y, v * T), cy.at[0]), (columns(core_y, (v + 1 - 2 * c) * T), cy.at[1]),
        (z_first, tz1), (z_second, tz2), (columns(y_first, v * T), ty1), (columns(y_third, v * T), ty3),
        (columns(x_second, u * T), tx2), (columns(x_third, u * T), tx3), (columns(core_x, u * T), cx),
    ]
    loads = [pltpu.make_async_copy(a, b, in_s.at[k]) for k, (a, b) in enumerate(loads)]
    own_copy(0).start()
    for load in loads:
        load.start()

    def start_own(ch, _):
        own_copy(ch).start()
        return 0

    lax.fori_loop(1, NCH, start_own, 0)

    @pl.when(lax.div(t, 4) == v)
    def _():
        pl.semaphore_wait(barrier, len(others) + 3)

    @pl.when(lax.div(t, 4) != v)
    def _():
        pl.semaphore_wait(barrier, len(others) + 4)

    par_copy(0).start()
    for load in loads[0:3]:
        load.wait()

    def r_of(row):
        h = jnp.where(row >= 48, 1, 0)
        rest = row - 48 * h
        e = rest & 15
        return 24 * (((e >> 2) & 1) * 4 + (e & 3)) + 12 * (e >> 3) + 6 * c + 3 * h + (rest >> 4)

    eye = pick(T, T, lambda row: row)
    gap = jnp.zeros((32, T), BF16)
    czt[...] = nn(pick(96, S, r_of), cz[...]).astype(BF16)
    for o in range(2):
        low, high = cy[o, 0:128], cy[o, 128:192]
        wy[0, o * T : o * T + T, :] = nt(eye, jnp.concatenate([low, high, gap, gap], axis=0)).astype(BF16)
        wy[1, o * T : o * T + T, :] = nt(eye, jnp.concatenate([low, gap, gap, high], axis=0)).astype(BF16)
    par_copy(1).start()

    def prepare():
        for load in loads[3:]:
            load.wait()
        zp[...] = nt(eye, jnp.concatenate([tz1[...], gap, tz2[...], gap], axis=0)).astype(BF16)
        y1[...] = nt(eye, jnp.concatenate([ty1[...], gap], axis=0))
        x2[...] = nt(eye, jnp.concatenate([tx2[...], gap], axis=0))
        turned = tx3[...].astype(F32)
        for n in range(T // MODE):
            x3[n, :, 0:MODE] = turned[:, n * MODE : n * MODE + MODE]
        cxp[...] = cx[...]
        fbuf[...] = jnp.zeros_like(fbuf)
        g2[...] = jnp.zeros_like(g2)
        g3[...] = jnp.zeros_like(g3)

    def contract_z(ch):
        own_copy(ch).wait()
        par_copy(ch).wait_recv()

        @pl.when(ch < NCH - 2)
        def _():
            par_copy(ch + 2).start()

        for a in range(CH):
            both = jnp.concatenate([own[ch, a], par[ch, a]], axis=0)
            w = nt(czt[...], both).astype(BF16)
            for h in range(2):
                for i in range(3):
                    at = (h * 3 + i) * 16
                    wt[h, i, ch, a * 16 : a * 16 + 16, :] = w[at : at + 16]

    def contract_y(n, k):
        ch, d, count = lax.rem(n, NCH), lax.rem(n, 2), len(PIECES[k])
        for b in range(CH // 8):
            made = {}
            for i in range(3):
                kinds = [kind for kind, index in PIECES[k] if index == i]
                if kinds:
                    first = wt[0, i, ch, b * 128 : b * 128 + 128, :]
                    other = wt[1, i, ch, b * 128 : b * 128 + 128, :]
                if kinds == [0, 1, 2]:
                    top, bot = nn(first, wy[0]), nn(other, wy[1])
                    made[0, i], made[1, i], made[2, i] = top[:, 0:128], bot[:, 0:128], top[:, 128:] + bot[:, 128:]
                elif kinds == [0, 1]:
                    made[0, i], made[1, i] = nn(first, wy[0, :, 0:128]), nn(other, wy[1, :, 0:128])
                elif kinds == [2]:
                    made[2, i] = nn(first, wy[0, :, 128:]) + nn(other, wy[1, :, 128:])
            for a in range(8):
                for m, piece in enumerate(PIECES[k]):
                    at = ((b * 8 + a) * count + m) * 16
                    us[at : at + 16, :] = made[piece][a * 16 : a * 16 + 16]
        for e in range(16):
            q = (1 - d) * e + d * ((e % 4) * 4 + e // 4)
            for m in range(count):
                lines = us[pl.ds(m * 16 + e, CH, stride=16 * count), :]
                send[n, q, m * CH : m * CH + CH, :] = lines.astype(BF16)
        if count == 1:
            opp_copy(n, CH).start()
            for w in range(2):
                all_copy(n, w, CH).start()
        else:
            for w in range(2):
                mid_copy(n, w, count * CH).start()

    def direct(n, k):
        if len(PIECES[k]) > 1:
            for w in range(2):
                dir_copy(n, w, len(PIECES[k]) * CH).start()

    def modes(n):
        ch, off = lax.div(n, 2), lax.rem(n, 2) * MODE
        rows = x2[pl.ds(pl.multiple_of(n * MODE, MODE), MODE), :]
        total = g2[...]
        factors = []
        for a in range(MODE):
            m = nn(own[ch, off + a], zp[...])
            g1[pl.ds(n * MODE + a, 1), :] = jnp.sum(m[:, 0:128] * y1[...], axis=0, keepdims=True)
            total = total + m[:, 128:] * rows[a : a + 1]
            factors.append((ty3[...].astype(F32) * x3[n, :, a : a + 1]).astype(BF16))
        g2[...] = total
        block = own[ch, pl.ds(off, MODE)].reshape(MODE * T, T)
        g3[...] += nn(jnp.concatenate(factors, axis=1), block)

    def forward(n, k):
        p, size = place(lax.rem(n, 2)), len(PIECES[k]) * CH
        if len(PIECES[k]) > 1:
            for w in range(2):
                mid_copy(n, w, size).wait_recv()
                base = step(p, 1 + 2 * w) * 4 + 2 * w
                for h in range(2):
                    mine = send[n, base + h, 0:size].astype(F32)
                    send[n, base + h, 0:size] = (mine + mid[n, 2 * w + h, 0:size].astype(F32)).astype(BF16)
                com_copy(n, w, size).start()

    def finish(n, k):
        p, size = place(lax.rem(n, 2)), len(PIECES[k]) * CH
        if len(PIECES[k]) > 1:
            for w in range(2):
                dir_copy(n, w, size).wait_recv()
                com_copy(n, w, size).wait_recv()
        else:
            opp_copy(n, size).wait_recv()
            for w in range(2):
                all_copy(n, w, size).wait_recv()
        for b in range(4):
            tot = send[n, p * 4 + b, 0:size].astype(F32) + ring[n, 0, b, 0:size].astype(F32)
            tot = tot + ring[n, 1, b, 0:size].astype(F32)
            if len(PIECES[k]) == 1:
                tot = tot + mid[n, b, 0:size].astype(F32)
            send[n, p * 4 + b, 0:size] = tot.astype(BF16)
        for o in (1, 2, 3):
            sec_copy(n, o, size).start()

    def collect(n, k):
        ch, d, size = lax.rem(n, NCH), lax.rem(n, 2), len(PIECES[k]) * CH
        for o in (1, 2, 3):
            sec_copy(n, o, size).wait_recv()
        tot = send[n, place(d) * 4 + place(1 - d), 0:size].astype(F32)
        for o in range(3):
            tot = tot + second[n, o, 0:size].astype(F32)
        tot = tot.astype(BF16)
        for m in range(len(PIECES[k])):
            gath[k, m, pl.ds(pl.multiple_of(ch * CH, CH), CH), :] = tot[m * CH : m * CH + CH]

    def drain(n, k):
        size = len(PIECES[k]) * CH
        if len(PIECES[k]) > 1:
            for w in range(2):
                mid_copy(n, w, size).wait_send()
                dir_copy(n, w, size).wait_send()
                com_copy(n, w, size).wait_send()
        else:
            opp_copy(n, size).wait_send()
            for w in range(2):
                all_copy(n, w, size).wait_send()
        for o in (1, 2, 3):
            sec_copy(n, o, size).wait_send()

    def unit(n, lag, act):
        m = n - lag

        for k in range(PARTS):

            @pl.when((m >= k * NCH) & (m < k * NCH + NCH))
            def _():
                act(m, k)

    def contract_x(i):
        parts = [nn(cxp[...], gath[i, m]).reshape(8, 24, T) for m in range(len(PIECES[i]))]
        if i == THIRD:
            parts.append(g3[...].reshape(8, 12, T))
        used = sum(p.shape[1] for p in parts)
        if used < lines(i):
            parts.append(jnp.zeros((8, lines(i) - used, T), F32))
        hbuf[i, :, 0 : lines(i), :] = jnp.concatenate(parts, axis=1).astype(BF16)
        for k in (4, 3, 5, 2, 6, 1, 7):
            z_copy(i, k).start()

    def finish_z(i):
        for k in range(1, 8):
            z_copy(i, k).wait_recv()
        tot = hbuf[i, z, 0 : lines(i), :].astype(F32)
        for k in range(7):
            tot = tot + zrecv[i, k, 0 : lines(i), :].astype(F32)
        for m in range(slabs(i)):
            each = 6 if m < len(PIECES[i]) else 3
            for q in range(4):
                at = m * 24 + q * each
                fbuf[i, q, m, 0:each] = tot[at : at + each]
        for k in (1, 2, 3):
            f_copy(i, k).start()

    def modes_a():
        high = lax.Precision.HIGHEST
        one = nn(pick(T, T, lambda q: 16 * ((q >> 1) & 7) + 2 * (q >> 4) + (q & 1), F32), g1[...], high)
        two = nn(pick(T, T, lambda q: 32 * ((q >> 2) & 3) + 4 * (q >> 4) + (q & 3), F32), g2[...], high)
        m12[:, 0:16, :] = one.reshape(8, 16, T).astype(BF16)
        m12[:, 16:32, :] = two.reshape(8, 16, T).astype(BF16)
        for k in range(1, 8):
            ma_copy(k).start()

    def modes_b():
        total = m12[g].astype(F32)
        for k in range(1, 8):
            ma_copy(k).wait_recv()
            total = total + arecv[k - 1].astype(F32)

        def source_row(q):
            i = q & 7
            low = jnp.where(i < 2, 2 * (q >> 3) + i, -1)
            return jnp.where(q < 64, low, jnp.where(i < 4, 16 + 4 * ((q - 64) >> 3) + i, -1))

        msg[...] = nn(pick(96, 32, source_row, F32), total, lax.Precision.HIGHEST).reshape(12, 8, T)
        for k in range(1, 8):
            mb_copy(k).start()
        for b in range(4):

            @pl.when(v * 4 + b != t)
            def _():
                mc_send(b).start()

            @pl.when(v * 4 + b == t)
            def _():
                r2[u] = msg[8 + b]

    def turn(n, _):
        @pl.when(n < NCH)
        def _():
            contract_z(n)

        @pl.when(n == MODE_0 - 1)
        def _():
            prepare()

        unit(n, 0, contract_y)
        unit(n, DIRECT, direct)
        unit(n, FORWARD, forward)

        @pl.when((n >= MODE_0) & (n < MODE_0 + T // MODE))
        def _():
            modes(n - MODE_0)

        unit(n, FINISH, finish)
        unit(n, COLLECT, collect)

        for i in range(PARTS):
            last = NCH * i + NCH - 1 + COLLECT

            @pl.when(n == last)
            def _():
                contract_x(i)

            if last + ZLAG < UNITS + COLLECT:

                @pl.when(n == last + ZLAG)
                def _():
                    finish_z(i)

        @pl.when(n == MODE_A)
        def _():
            modes_a()

        @pl.when(n == MODE_B)
        def _():
            modes_b()

        return 0

    lax.fori_loop(0, UNITS + COLLECT, turn, 0)

    def sent(n, _):
        unit(n, 0, drain)
        return 0

    lax.fori_loop(0, UNITS, sent, 0)
    for ch in range(NCH):
        par_copy(ch).wait_send()
    for k in range(1, 8):
        ma_copy(k).wait_send()

    def place_rows(i):
        for m, (kind, index) in enumerate(PIECES[i]):
            out[s * 9 + kind * 3 + index] = fbuf[i, s, m]
        for k in (1, 2, 3):
            f_copy(i, k).wait_recv()
            for m, (kind, index) in enumerate(PIECES[i]):
                out[step(s, 4 - k) * 9 + kind * 3 + index] = frecv[i, k - 1, m]
        if i == THIRD:
            at = len(PIECES[i])
            out[36] = fbuf[i, s, at] + frecv[i, 0, at] + frecv[i, 1, at] + frecv[i, 2, at]

    def drain_rows(i):
        for k in range(1, 8):
            z_copy(i, k).wait_send()
        for k in (1, 2, 3):
            f_copy(i, k).wait_send()

    for i in range(PARTS - 1):
        if NCH * i + NCH - 1 + ZLAG >= UNITS:
            finish_z(i)

    first = msg[v]
    for k in range(1, 8):
        mb_copy(k).wait_recv()
        first = first + r1[k - 1]
    out[37] = first
    for k in range(4):

        @pl.when(k * 8 + lax.div(t, 4) != t)
        def _():
            mc_recv(k).wait_recv()

    out[38] = r2[0] + r2[1] + r2[2] + r2[3]
    for k in range(1, 8):
        mb_copy(k).wait_send()
    for b in range(4):

        @pl.when(v * 4 + b != t)
        def _():
            mc_send(b).wait_send()

    for i in range(PARTS - 1):
        place_rows(i)
        drain_rows(i)
    finish_z(PARTS - 1)
    place_rows(PARTS - 1)
    drain_rows(PARTS - 1)


def outputs_kernel(x, one, two, three, core):
    one[...] = x[37 * 8 : 37 * 8 + 2, 0:K]
    two[...] = x[38 * 8 : 38 * 8 + 4, 0:K]
    three[...] = x[36 * 8 : 36 * 8 + 3, :]
    for p in range(6):
        rows = x[pl.ds(p, 36, stride=8), :]
        for q in range(4):
            core[p, 6 * q : 6 * q + 6, 0:128] = rows[9 * q : 9 * q + 6]
            core[p, 6 * q : 6 * q + 3, 128:192] = rows[9 * q + 6 : 9 * q + 9, 0:64]
            core[p, 6 * q + 3 : 6 * q + 6, 128:192] = rows[9 * q + 6 : 9 * q + 9, 64:128]


def shards(field, *small):
    vm, hbm = pl.BlockSpec(memory_space=pltpu.VMEM), pl.BlockSpec(memory_space=pl.ANY)
    dma, mem = pltpu.SemaphoreType.DMA, pltpu.VMEM
    unit = [dma((UNITS, 2))] * 6 + [dma((UNITS, 3))] * 2
    raw = pl.pallas_call(
        main_kernel,
        out_shape=jax.ShapeDtypeStruct((39, 8, 128), F32),
        in_specs=[hbm] * 10,
        out_specs=vm,
        scratch_shapes=[
            mem((NCH, CH, T, T), BF16),
            mem((NCH, CH, T, T), BF16),
            mem((2, 3, NCH, CH * 16, 256), BF16),
            mem((CH * 16 * MOST, 128), F32),
            mem((UNITS, 16, ROWS, 128), BF16),
            mem((UNITS, 4, ROWS, 128), BF16),
            mem((UNITS, 2, 4, ROWS, 128), BF16),
            mem((UNITS, 3, ROWS, 128), BF16),
            mem((PARTS, MOST, T, 128), BF16),
            mem((PARTS, 8, 32 * MOST + 32, 128), BF16),
            mem((PARTS, 7, 32 * MOST + 32, 128), BF16),
            mem((PARTS, 4, MOST + 1, 8, 128), F32),
            mem((PARTS, 3, MOST + 1, 8, 128), F32),
            mem((S, T), BF16), mem((2, S, T), BF16), mem((S, T), BF16),
            mem((K, T), BF16), mem((K, T), BF16), mem((K, T), BF16), mem((K, T), BF16),
            mem((K, T), BF16), mem((K, T), BF16),
            mem((K, T), BF16),
            mem((S, T), BF16),
            mem((2, 2 * T, 256), BF16),
            mem((T, 256), BF16),
            mem((T, 128), F32), mem((T, 128), F32),
            mem((T // MODE, K, 128), F32),
            mem((T, 128), F32), mem((T, 128), F32), mem((K, T), F32),
            mem((8, 32, 128), BF16), mem((7, 32, 128), BF16),
            mem((12, 8, 128), F32), mem((7, 8, 128), F32), mem((4, 8, 128), F32),
            dma((10,)), dma((NCH,)), dma((NCH,)), dma((NCH,)),
            *unit,
            dma((PARTS, 7)), dma((PARTS, 7)), dma((PARTS, 3)), dma((PARTS, 3)),
            dma((7,)), dma((7,)), dma((7,)), dma((7,)), dma((4,)), dma((4,)),
        ],
        compiler_params=pltpu.CompilerParams(
            collective_id=0, has_side_effects=True, vmem_limit_bytes=56 * 1024 * 1024
        ),
    )(field, *[x.T for x in small])
    one, two, three, core = pl.pallas_call(
        outputs_kernel,
        out_shape=(
            jax.ShapeDtypeStruct((2, K), F32),
            jax.ShapeDtypeStruct((4, K), F32),
            jax.ShapeDtypeStruct((3, T), F32),
            jax.ShapeDtypeStruct((6, 24, S), F32),
        ),
        in_specs=[vm],
        out_specs=(vm, vm, vm, vm),
    )(raw.reshape(39 * 8, 128))
    return (one, two, three, core.transpose(0, 2, 1))


def solution(mesh):
    return jax.shard_map(
        shards,
        mesh=mesh,
        in_specs=(
            P("xy", None, None, "gz"),
            P(), P(), P("gz", None), P(), P(), P(), P(), P("gz", None), P("gz", None),
        ),
        out_specs=(
            P(("xy", "gz"), None),
            P(("xy", "gz"), None),
            P("xy", "gz"),
            P("xy", None, "gz"),
        ),
        check_vma=False,
    )
```

```python
import jax
import jax.numpy as jnp
from jax import lax
from jax.experimental import pallas as pl
from jax.experimental.pallas import tpu as pltpu
from jax.sharding import PartitionSpec as P

MESH = pl.DeviceIdType.MESH
F32, BF16, I32 = jnp.float32, jnp.bfloat16, jnp.int32
K = 96
S = 192
T = 128
CH = 32
NCH = T // CH
PIECES = (((0, 0), (1, 0), (2, 0)), ((0, 1), (1, 1), (2, 1)), ((0, 2), (1, 2), (2, 2)))
THIRD = 1
PARTS = len(PIECES)
UNITS = PARTS * NCH
MOST = 3
ROWS = MOST * CH
MODE = 16
DIRECT, FORWARD, FINISH, COLLECT, ZLAG = 1, 2, 5, 8, 5
MODE_0, MODE_A, MODE_B = 5, 13, 16


def nn(a, b, precision=None):
    return lax.dot_general(a, b, (((1,), (0,)), ((), ())), preferred_element_type=F32, precision=precision)


def nt(a, b):
    return lax.dot_general(a, b, (((1,), (1,)), ((), ())), preferred_element_type=F32)


def pick(rows, columns, column_of, dtype=BF16):
    r = lax.broadcasted_iota(I32, (rows, columns), 0)
    return jnp.where(lax.broadcasted_iota(I32, (rows, columns), 1) == column_of(r), 1.0, 0.0).astype(dtype)


def main_kernel(
    field, core_x, core_y, core_z, x_second, x_third, y_first, y_third, z_first, z_second,
    out,
    own, par, wt, us, send, mid, ring, second, gath, hbuf, zrecv, fbuf, frecv,
    cx, cy, cz, tx2, tx3, ty1, ty3, tz1, tz2,
    czt, cxp, wy, zp, y1, x2, x3, g1, g2, g3, m12, arecv, msg, r1, r2,
    in_s, own_sem, par_s, par_r, mid_s, mid_r, dir_s, dir_r, com_s, com_r, sec_s, sec_r, z_s, z_r, f_s, f_r,
    ma_s, ma_r, mb_s, mb_r, mc_s, mc_r,
):
    t, g = lax.axis_index("xy"), lax.axis_index("gz")
    z, s = lax.div(t, 4), lax.rem(t, 4)
    xh, c = lax.div(s, 2), lax.rem(s, 2)
    xl, y = lax.div(g, 4), lax.rem(g, 4)
    X = xh * 2 + xl
    u, v = lax.div(t, 8), lax.rem(t, 8)
    mate = t + 1 - 2 * c

    def ring_dev(d, q):
        tt = t + (1 - d) * 2 * (lax.div(q, 2) - xh)
        gg = g + (1 - d) * 4 * (lax.rem(q, 2) - xl) + d * (q - y)
        return (tt, gg)

    def place(d):
        return (1 - d) * X + d * y

    def step(p, k):
        return lax.rem(p + k, 4)

    def copy(src, dst, ss, rs, dev):
        return pltpu.make_async_remote_copy(
            src_ref=src, dst_ref=dst, send_sem=ss, recv_sem=rs, device_id=dev, device_id_type=MESH
        )

    def own_copy(ch):
        return pltpu.make_async_copy(field.at[0, pl.ds(ch * CH, CH)], own.at[ch], own_sem.at[ch])

    def par_copy(ch):
        return copy(field.at[0, pl.ds(ch * CH, CH)], par.at[ch], par_s.at[ch], par_r.at[ch], (mate, g))

    def block(n, place_of, size):
        return send.at[n, place_of, pl.ds(0, size)]

    def mid_copy(n, w, size):
        d = lax.rem(n, 2)
        p = place(d)
        src, dst = block(n, pl.ds(step(p, 2) * 4 + 2 * w, 2), size), mid.at[n, pl.ds(2 * w, 2), pl.ds(0, size)]
        return copy(src, dst, mid_s.at[n, w], mid_r.at[n, w], ring_dev(d, step(p, 1 + 2 * w)))

    def opp_copy(n, size):
        d = lax.rem(n, 2)
        q = step(place(d), 2)
        src, dst = block(n, pl.ds(q * 4, 4), size), mid.at[n, pl.ds(0, 4), pl.ds(0, size)]
        return copy(src, dst, mid_s.at[n, 0], mid_r.at[n, 0], ring_dev(d, q))

    def near_copy(n, w, h, count, size, ss, rs):
        d = lax.rem(n, 2)
        q = step(place(d), 1 + 2 * w)
        src, dst = block(n, pl.ds(q * 4 + h, count), size), ring.at[n, w, pl.ds(h, count), pl.ds(0, size)]
        return copy(src, dst, ss.at[n, w], rs.at[n, w], ring_dev(d, q))

    def dir_copy(n, w, size):
        return near_copy(n, w, 2 * (1 - w), 2, size, dir_s, dir_r)

    def com_copy(n, w, size):
        return near_copy(n, w, 2 * w, 2, size, com_s, com_r)

    def all_copy(n, w, size):
        return near_copy(n, w, 0, 4, size, dir_s, dir_r)

    def sec_copy(n, k, size):
        d = lax.rem(n, 2)
        q = step(place(1 - d), k)
        src, dst = block(n, place(d) * 4 + q, size), second.at[n, k - 1, pl.ds(0, size)]
        return copy(src, dst, sec_s.at[n, k - 1], sec_r.at[n, k - 1], ring_dev(1 - d, q))

    def slabs(i):
        return len(PIECES[i]) + (i == THIRD)

    def lines(i):
        used = 24 * len(PIECES[i]) + (12 if i == THIRD else 0)
        return (used + 15) // 16 * 16

    def z_copy(i, k):
        zz = lax.rem(z + k, 8)
        size = lines(i)
        src, dst = hbuf.at[i, zz, pl.ds(0, size)], zrecv.at[i, k - 1, pl.ds(0, size)]
        return copy(src, dst, z_s.at[i, k - 1], z_r.at[i, k - 1], (zz * 4 + s, g))

    def f_copy(i, k):
        q = step(s, k)
        size = slabs(i)
        src, dst = fbuf.at[i, q, pl.ds(0, size)], frecv.at[i, k - 1, pl.ds(0, size)]
        return copy(src, dst, f_s.at[i, k - 1], f_r.at[i, k - 1], (z * 4 + q, g))

    def ma_copy(k):
        q = lax.rem(g + k, 8)
        return copy(m12.at[q], arecv.at[k - 1], ma_s.at[k - 1], ma_r.at[k - 1], (t, q))

    def mb_copy(k):
        q = lax.rem(v + k, 8)
        return copy(msg.at[q], r1.at[k - 1], mb_s.at[k - 1], mb_r.at[k - 1], (u * 8 + q, g))

    def mc_send(b):
        return copy(msg.at[8 + b], r2.at[u], mc_s.at[b], mc_r.at[u], (v * 4 + b, g))

    def mc_recv(k):
        return copy(msg.at[8], r2.at[k], mc_s.at[0], mc_r.at[k], (k * 8 + lax.div(t, 4), g))

    barrier = pltpu.get_barrier_semaphore()
    others = [ring_dev(0, step(X, 3 - 2 * xl))]
    others += [(z * 4 + step(s, k), g) for k in (1, 2, 3)]
    others += [(t, lax.rem(g + k, 8)) for k in range(1, 8)]
    others += [(lax.rem(z + k, 8) * 4 + s, g) for k in range(1, 8)]
    others += [((z + 1 - 2 * lax.rem(z, 2)) * 4 + step(s, k), g) for k in (1, 2, 3)]
    for dev in others:
        pl.semaphore_signal(barrier, inc=1, device_id=dev, device_id_type=MESH)
    for k in range(4):
        source = k * 8 + lax.div(t, 4)

        @pl.when(source != t)
        def _():
            pl.semaphore_signal(barrier, inc=1, device_id=(source, g), device_id_type=MESH)

    def columns(ref, base):
        return ref.at[:, pl.ds(pl.multiple_of(base, T), T)]

    loads = [
        (core_z, cz), (columns(core_y, v * T), cy.at[0]), (columns(core_y, (v + 1 - 2 * c) * T), cy.at[1]),
        (z_first, tz1), (z_second, tz2), (columns(y_first, v * T), ty1), (columns(y_third, v * T), ty3),
        (columns(x_second, u * T), tx2), (columns(x_third, u * T), tx3), (columns(core_x, u * T), cx),
    ]
    loads = [pltpu.make_async_copy(a, b, in_s.at[k]) for k, (a, b) in enumerate(loads)]
    own_copy(0).start()
    for load in loads:
        load.start()

    def start_own(ch, _):
        own_copy(ch).start()
        return 0

    lax.fori_loop(1, NCH, start_own, 0)

    @pl.when(lax.div(t, 4) == v)
    def _():
        pl.semaphore_wait(barrier, len(others) + 3)

    @pl.when(lax.div(t, 4) != v)
    def _():
        pl.semaphore_wait(barrier, len(others) + 4)

    par_copy(0).start()
    for load in loads[0:3]:
        load.wait()

    def r_of(row):
        h = jnp.where(row >= 48, 1, 0)
        rest = row - 48 * h
        e = rest & 15
        return 24 * (((e >> 2) & 1) * 4 + (e & 3)) + 12 * (e >> 3) + 6 * c + 3 * h + (rest >> 4)

    eye = pick(T, T, lambda row: row)
    gap = jnp.zeros((32, T), BF16)
    czt[...] = nn(pick(96, S, r_of), cz[...]).astype(BF16)
    for o in range(2):
        low, high = cy[o, 0:128], cy[o, 128:192]
        wy[0, o * T : o * T + T, :] = nt(eye, jnp.concatenate([low, high, gap, gap], axis=0)).astype(BF16)
        wy[1, o * T : o * T + T, :] = nt(eye, jnp.concatenate([low, gap, gap, high], axis=0)).astype(BF16)
    par_copy(1).start()

    def prepare():
        for load in loads[3:]:
            load.wait()
        zp[...] = nt(eye, jnp.concatenate([tz1[...], gap, tz2[...], gap], axis=0)).astype(BF16)
        y1[...] = nt(eye, jnp.concatenate([ty1[...], gap], axis=0))
        x2[...] = nt(eye, jnp.concatenate([tx2[...], gap], axis=0))
        turned = tx3[...].astype(F32)
        for n in range(T // MODE):
            x3[n, :, 0:MODE] = turned[:, n * MODE : n * MODE + MODE]
        cxp[...] = cx[...]
        fbuf[...] = jnp.zeros_like(fbuf)
        g2[...] = jnp.zeros_like(g2)
        g3[...] = jnp.zeros_like(g3)

    def contract_z(ch):
        own_copy(ch).wait()
        par_copy(ch).wait_recv()

        @pl.when(ch < NCH - 2)
        def _():
            par_copy(ch + 2).start()

        for a in range(CH):
            both = jnp.concatenate([own[ch, a], par[ch, a]], axis=0)
            w = nt(czt[...], both).astype(BF16)
            for h in range(2):
                for i in range(3):
                    at = (h * 3 + i) * 16
                    wt[h, i, ch, a * 16 : a * 16 + 16, :] = w[at : at + 16]

    def contract_y(n, k):
        ch, d, count = lax.rem(n, NCH), lax.rem(n, 2), len(PIECES[k])
        for b in range(CH // 8):
            made = {}
            for i in range(3):
                kinds = [kind for kind, index in PIECES[k] if index == i]
                if kinds:
                    first = wt[0, i, ch, b * 128 : b * 128 + 128, :]
                    other = wt[1, i, ch, b * 128 : b * 128 + 128, :]
                if kinds == [0, 1, 2]:
                    top, bot = nn(first, wy[0]), nn(other, wy[1])
                    made[0, i], made[1, i], made[2, i] = top[:, 0:128], bot[:, 0:128], top[:, 128:] + bot[:, 128:]
                elif kinds == [0, 1]:
                    made[0, i], made[1, i] = nn(first, wy[0, :, 0:128]), nn(other, wy[1, :, 0:128])
                elif kinds == [2]:
                    made[2, i] = nn(first, wy[0, :, 128:]) + nn(other, wy[1, :, 128:])
            for a in range(8):
                for m, piece in enumerate(PIECES[k]):
                    at = ((b * 8 + a) * count + m) * 16
                    us[at : at + 16, :] = made[piece][a * 16 : a * 16 + 16]
        for e in range(16):
            q = (1 - d) * e + d * ((e % 4) * 4 + e // 4)
            for m in range(count):
                lines = us[pl.ds(m * 16 + e, CH, stride=16 * count), :]
                send[n, q, m * CH : m * CH + CH, :] = lines.astype(BF16)
        if count == 1:
            opp_copy(n, CH).start()
            for w in range(2):
                all_copy(n, w, CH).start()
        else:
            for w in range(2):
                mid_copy(n, w, count * CH).start()

    def direct(n, k):
        if len(PIECES[k]) > 1:
            for w in range(2):
                dir_copy(n, w, len(PIECES[k]) * CH).start()

    def modes(n):
        ch, off = lax.div(n, 2), lax.rem(n, 2) * MODE
        rows = x2[pl.ds(pl.multiple_of(n * MODE, MODE), MODE), :]
        total = g2[...]
        factors = []
        for a in range(MODE):
            m = nn(own[ch, off + a], zp[...])
            g1[pl.ds(n * MODE + a, 1), :] = jnp.sum(m[:, 0:128] * y1[...], axis=0, keepdims=True)
            total = total + m[:, 128:] * rows[a : a + 1]
            factors.append((ty3[...].astype(F32) * x3[n, :, a : a + 1]).astype(BF16))
        g2[...] = total
        block = own[ch, pl.ds(off, MODE)].reshape(MODE * T, T)
        g3[...] += nn(jnp.concatenate(factors, axis=1), block)

    def forward(n, k):
        p, size = place(lax.rem(n, 2)), len(PIECES[k]) * CH
        if len(PIECES[k]) > 1:
            for w in range(2):
                mid_copy(n, w, size).wait_recv()
                base = step(p, 1 + 2 * w) * 4 + 2 * w
                for h in range(2):
                    mine = send[n, base + h, 0:size].astype(F32)
                    send[n, base + h, 0:size] = (mine + mid[n, 2 * w + h, 0:size].astype(F32)).astype(BF16)
                com_copy(n, w, size).start()

    def finish(n, k):
        p, size = place(lax.rem(n, 2)), len(PIECES[k]) * CH
        if len(PIECES[k]) > 1:
            for w in range(2):
                dir_copy(n, w, size).wait_recv()
                com_copy(n, w, size).wait_recv()
        else:
            opp_copy(n, size).wait_recv()
            for w in range(2):
                all_copy(n, w, size).wait_recv()
        for b in range(4):
            tot = send[n, p * 4 + b, 0:size].astype(F32) + ring[n, 0, b, 0:size].astype(F32)
            tot = tot + ring[n, 1, b, 0:size].astype(F32)
            if len(PIECES[k]) == 1:
                tot = tot + mid[n, b, 0:size].astype(F32)
            send[n, p * 4 + b, 0:size] = tot.astype(BF16)
        for o in (1, 2, 3):
            sec_copy(n, o, size).start()

    def collect(n, k):
        ch, d, size = lax.rem(n, NCH), lax.rem(n, 2), len(PIECES[k]) * CH
        for o in (1, 2, 3):
            sec_copy(n, o, size).wait_recv()
        tot = send[n, place(d) * 4 + place(1 - d), 0:size].astype(F32)
        for o in range(3):
            tot = tot + second[n, o, 0:size].astype(F32)
        tot = tot.astype(BF16)
        for m in range(len(PIECES[k])):
            gath[k, m, pl.ds(pl.multiple_of(ch * CH, CH), CH), :] = tot[m * CH : m * CH + CH]

    def drain(n, k):
        size = len(PIECES[k]) * CH
        if len(PIECES[k]) > 1:
            for w in range(2):
                mid_copy(n, w, size).wait_send()
                dir_copy(n, w, size).wait_send()
                com_copy(n, w, size).wait_send()
        else:
            opp_copy(n, size).wait_send()
            for w in range(2):
                all_copy(n, w, size).wait_send()
        for o in (1, 2, 3):
            sec_copy(n, o, size).wait_send()

    def unit(n, lag, act):
        m = n - lag

        for k in range(PARTS):

            @pl.when((m >= k * NCH) & (m < k * NCH + NCH))
            def _():
                act(m, k)

    def contract_x(i):
        parts = [nn(cxp[...], gath[i, m]).reshape(8, 24, T) for m in range(len(PIECES[i]))]
        if i == THIRD:
            parts.append(g3[...].reshape(8, 12, T))
        used = sum(p.shape[1] for p in parts)
        if used < lines(i):
            parts.append(jnp.zeros((8, lines(i) - used, T), F32))
        hbuf[i, :, 0 : lines(i), :] = jnp.concatenate(parts, axis=1).astype(BF16)
        for k in (4, 3, 5, 2, 6, 1, 7):
            z_copy(i, k).start()

    def finish_z(i):
        for k in range(1, 8):
            z_copy(i, k).wait_recv()
        tot = hbuf[i, z, 0 : lines(i), :].astype(F32)
        for k in range(7):
            tot = tot + zrecv[i, k, 0 : lines(i), :].astype(F32)
        for m in range(slabs(i)):
            each = 6 if m < len(PIECES[i]) else 3
            for q in range(4):
                at = m * 24 + q * each
                fbuf[i, q, m, 0:each] = tot[at : at + each]
        for k in (1, 2, 3):
            f_copy(i, k).start()

    def modes_a():
        high = lax.Precision.HIGHEST
        one = nn(pick(T, T, lambda q: 16 * ((q >> 1) & 7) + 2 * (q >> 4) + (q & 1), F32), g1[...], high)
        two = nn(pick(T, T, lambda q: 32 * ((q >> 2) & 3) + 4 * (q >> 4) + (q & 3), F32), g2[...], high)
        m12[:, 0:16, :] = one.reshape(8, 16, T).astype(BF16)
        m12[:, 16:32, :] = two.reshape(8, 16, T).astype(BF16)
        for k in range(1, 8):
            ma_copy(k).start()

    def modes_b():
        total = m12[g].astype(F32)
        for k in range(1, 8):
            ma_copy(k).wait_recv()
            total = total + arecv[k - 1].astype(F32)

        def source_row(q):
            i = q & 7
            low = jnp.where(i < 2, 2 * (q >> 3) + i, -1)
            return jnp.where(q < 64, low, jnp.where(i < 4, 16 + 4 * ((q - 64) >> 3) + i, -1))

        msg[...] = nn(pick(96, 32, source_row, F32), total, lax.Precision.HIGHEST).reshape(12, 8, T)
        for k in range(1, 8):
            mb_copy(k).start()
        for b in range(4):

            @pl.when(v * 4 + b != t)
            def _():
                mc_send(b).start()

            @pl.when(v * 4 + b == t)
            def _():
                r2[u] = msg[8 + b]

    def turn(n, _):
        @pl.when(n < NCH)
        def _():
            contract_z(n)

        @pl.when(n == MODE_0 - 1)
        def _():
            prepare()

        unit(n, 0, contract_y)
        unit(n, DIRECT, direct)
        unit(n, FORWARD, forward)

        @pl.when((n >= MODE_0) & (n < MODE_0 + T // MODE))
        def _():
            modes(n - MODE_0)

        unit(n, FINISH, finish)
        unit(n, COLLECT, collect)

        for i in range(PARTS):
            last = NCH * i + NCH - 1 + COLLECT

            @pl.when(n == last)
            def _():
                contract_x(i)

            if last + ZLAG < UNITS + COLLECT:

                @pl.when(n == last + ZLAG)
                def _():
                    finish_z(i)

        @pl.when(n == MODE_A)
        def _():
            modes_a()

        @pl.when(n == MODE_B)
        def _():
            modes_b()

        return 0

    lax.fori_loop(0, UNITS + COLLECT, turn, 0)

    def sent(n, _):
        unit(n, 0, drain)
        return 0

    lax.fori_loop(0, UNITS, sent, 0)
    for ch in range(NCH):
        par_copy(ch).wait_send()
    for k in range(1, 8):
        ma_copy(k).wait_send()

    def place_rows(i):
        for m, (kind, index) in enumerate(PIECES[i]):
            out[s * 9 + kind * 3 + index] = fbuf[i, s, m]
        for k in (1, 2, 3):
            f_copy(i, k).wait_recv()
            for m, (kind, index) in enumerate(PIECES[i]):
                out[step(s, 4 - k) * 9 + kind * 3 + index] = frecv[i, k - 1, m]
        if i == THIRD:
            at = len(PIECES[i])
            out[36] = fbuf[i, s, at] + frecv[i, 0, at] + frecv[i, 1, at] + frecv[i, 2, at]

    def drain_rows(i):
        for k in range(1, 8):
            z_copy(i, k).wait_send()
        for k in (1, 2, 3):
            f_copy(i, k).wait_send()

    for i in range(PARTS - 1):
        if NCH * i + NCH - 1 + ZLAG >= UNITS:
            finish_z(i)

    first = msg[v]
    for k in range(1, 8):
        mb_copy(k).wait_recv()
        first = first + r1[k - 1]
    out[37] = first
    for k in range(4):

        @pl.when(k * 8 + lax.div(t, 4) != t)
        def _():
            mc_recv(k).wait_recv()

    out[38] = r2[0] + r2[1] + r2[2] + r2[3]
    for k in range(1, 8):
        mb_copy(k).wait_send()
    for b in range(4):

        @pl.when(v * 4 + b != t)
        def _():
            mc_send(b).wait_send()

    for i in range(PARTS - 1):
        place_rows(i)
        drain_rows(i)
    finish_z(PARTS - 1)
    place_rows(PARTS - 1)
    drain_rows(PARTS - 1)


def outputs_kernel(x, one, two, three, core):
    one[...] = x[37 * 8 : 37 * 8 + 2, 0:K]
    two[...] = x[38 * 8 : 38 * 8 + 4, 0:K]
    three[...] = x[36 * 8 : 36 * 8 + 3, :]
    for p in range(6):
        rows = x[pl.ds(p, 36, stride=8), :]
        for q in range(4):
            core[p, 6 * q : 6 * q + 6, 0:128] = rows[9 * q : 9 * q + 6]
            core[p, 6 * q : 6 * q + 3, 128:192] = rows[9 * q + 6 : 9 * q + 9, 0:64]
            core[p, 6 * q + 3 : 6 * q + 6, 128:192] = rows[9 * q + 6 : 9 * q + 9, 64:128]


def shards(field, *small):
    vm, hbm = pl.BlockSpec(memory_space=pltpu.VMEM), pl.BlockSpec(memory_space=pl.ANY)
    dma, mem = pltpu.SemaphoreType.DMA, pltpu.VMEM
    unit = [dma((UNITS, 2))] * 6 + [dma((UNITS, 3))] * 2
    raw = pl.pallas_call(
        main_kernel,
        out_shape=jax.ShapeDtypeStruct((39, 8, 128), F32),
        in_specs=[hbm] * 10,
        out_specs=vm,
        scratch_shapes=[
            mem((NCH, CH, T, T), BF16),
            mem((NCH, CH, T, T), BF16),
            mem((2, 3, NCH, CH * 16, 256), BF16),
            mem((CH * 16 * MOST, 128), F32),
            mem((UNITS, 16, ROWS, 128), BF16),
            mem((UNITS, 4, ROWS, 128), BF16),
            mem((UNITS, 2, 4, ROWS, 128), BF16),
            mem((UNITS, 3, ROWS, 128), BF16),
            mem((PARTS, MOST, T, 128), BF16),
            mem((PARTS, 8, 32 * MOST + 32, 128), BF16),
            mem((PARTS, 7, 32 * MOST + 32, 128), BF16),
            mem((PARTS, 4, MOST + 1, 8, 128), F32),
            mem((PARTS, 3, MOST + 1, 8, 128), F32),
            mem((S, T), BF16), mem((2, S, T), BF16), mem((S, T), BF16),
            mem((K, T), BF16), mem((K, T), BF16), mem((K, T), BF16), mem((K, T), BF16),
            mem((K, T), BF16), mem((K, T), BF16),
            mem((K, T), BF16),
            mem((S, T), BF16),
            mem((2, 2 * T, 256), BF16),
            mem((T, 256), BF16),
            mem((T, 128), F32), mem((T, 128), F32),
            mem((T // MODE, K, 128), F32),
            mem((T, 128), F32), mem((T, 128), F32), mem((K, T), F32),
            mem((8, 32, 128), BF16), mem((7, 32, 128), BF16),
            mem((12, 8, 128), F32), mem((7, 8, 128), F32), mem((4, 8, 128), F32),
            dma((10,)), dma((NCH,)), dma((NCH,)), dma((NCH,)),
            *unit,
            dma((PARTS, 7)), dma((PARTS, 7)), dma((PARTS, 3)), dma((PARTS, 3)),
            dma((7,)), dma((7,)), dma((7,)), dma((7,)), dma((4,)), dma((4,)),
        ],
        compiler_params=pltpu.CompilerParams(
            collective_id=0, has_side_effects=True, vmem_limit_bytes=56 * 1024 * 1024
        ),
    )(field, *[x.T for x in small])
    one, two, three, core = pl.pallas_call(
        outputs_kernel,
        out_shape=(
            jax.ShapeDtypeStruct((2, K), F32),
            jax.ShapeDtypeStruct((4, K), F32),
            jax.ShapeDtypeStruct((3, T), F32),
            jax.ShapeDtypeStruct((6, 24, S), F32),
        ),
        in_specs=[vm],
        out_specs=(vm, vm, vm, vm),
    )(raw.reshape(39 * 8, 128))
    return (one, two, three, core.transpose(0, 2, 1))


def solution(mesh):
    return jax.shard_map(
        shards,
        mesh=mesh,
        in_specs=(
            P("xy", None, None, "gz"),
            P(), P(), P("gz", None), P(), P(), P(), P(), P("gz", None), P("gz", None),
        ),
        out_specs=(
            P(("xy", "gz"), None),
            P(("xy", "gz"), None),
            P("xy", "gz"),
            P("xy", None, "gz"),
        ),
        check_vma=False,
    )
```

```python
import jax
import jax.numpy as jnp
from jax import lax
from jax.experimental import pallas as pl
from jax.experimental.pallas import tpu as pltpu
from jax.sharding import PartitionSpec as P

MESH = pl.DeviceIdType.MESH
F32, BF16, I32 = jnp.float32, jnp.bfloat16, jnp.int32
K = 96
S = 192
T = 128
CH = 32
NCH = T // CH
PIECES = (((0, 0), (1, 0), (2, 0)), ((0, 1), (1, 1), (2, 1)), ((0, 2), (1, 2), (2, 2)))
THIRD = 1
PARTS = len(PIECES)
UNITS = PARTS * NCH
MOST = 3
ROWS = MOST * CH
MODE = 16
DIRECT, FORWARD, FINISH, COLLECT, ZLAG = 1, 2, 5, 8, 5
MODE_0, MODE_A, MODE_B = 5, 13, 16


def nn(a, b, precision=None):
    return lax.dot_general(a, b, (((1,), (0,)), ((), ())), preferred_element_type=F32, precision=precision)


def nt(a, b):
    return lax.dot_general(a, b, (((1,), (1,)), ((), ())), preferred_element_type=F32)


def pick(rows, columns, column_of, dtype=BF16):
    r = lax.broadcasted_iota(I32, (rows, columns), 0)
    return jnp.where(lax.broadcasted_iota(I32, (rows, columns), 1) == column_of(r), 1.0, 0.0).astype(dtype)


def main_kernel(
    field, core_x, core_y, core_z, x_second, x_third, y_first, y_third, z_first, z_second,
    out,
    own, par, wt, us, send, mid, ring, second, gath, hbuf, zrecv, fbuf, frecv,
    cx, cy, cz, tx2, tx3, ty1, ty3, tz1, tz2,
    czt, cxp, wy, zp, y1, x2, x3, g1, g2, g3, m12, arecv, msg, r1, r2,
    in_s, own_sem, par_s, par_r, mid_s, mid_r, dir_s, dir_r, com_s, com_r, sec_s, sec_r, z_s, z_r, f_s, f_r,
    ma_s, ma_r, mb_s, mb_r, mc_s, mc_r,
):
    t, g = lax.axis_index("xy"), lax.axis_index("gz")
    z, s = lax.div(t, 4), lax.rem(t, 4)
    xh, c = lax.div(s, 2), lax.rem(s, 2)
    xl, y = lax.div(g, 4), lax.rem(g, 4)
    X = xh * 2 + xl
    u, v = lax.div(t, 8), lax.rem(t, 8)
    mate = t + 1 - 2 * c

    def ring_dev(d, q):
        tt = t + (1 - d) * 2 * (lax.div(q, 2) - xh)
        gg = g + (1 - d) * 4 * (lax.rem(q, 2) - xl) + d * (q - y)
        return (tt, gg)

    def place(d):
        return (1 - d) * X + d * y

    def step(p, k):
        return lax.rem(p + k, 4)

    def copy(src, dst, ss, rs, dev):
        return pltpu.make_async_remote_copy(
            src_ref=src, dst_ref=dst, send_sem=ss, recv_sem=rs, device_id=dev, device_id_type=MESH
        )

    def own_copy(ch):
        return pltpu.make_async_copy(field.at[0, pl.ds(ch * CH, CH)], own.at[ch], own_sem.at[ch])

    def par_copy(ch):
        return copy(field.at[0, pl.ds(ch * CH, CH)], par.at[ch], par_s.at[ch], par_r.at[ch], (mate, g))

    def block(n, place_of, size):
        return send.at[n, place_of, pl.ds(0, size)]

    def mid_copy(n, w, size):
        d = lax.rem(n, 2)
        p = place(d)
        src, dst = block(n, pl.ds(step(p, 2) * 4 + 2 * w, 2), size), mid.at[n, pl.ds(2 * w, 2), pl.ds(0, size)]
        return copy(src, dst, mid_s.at[n, w], mid_r.at[n, w], ring_dev(d, step(p, 1 + 2 * w)))

    def opp_copy(n, size):
        d = lax.rem(n, 2)
        q = step(place(d), 2)
        src, dst = block(n, pl.ds(q * 4, 4), size), mid.at[n, pl.ds(0, 4), pl.ds(0, size)]
        return copy(src, dst, mid_s.at[n, 0], mid_r.at[n, 0], ring_dev(d, q))

    def near_copy(n, w, h, count, size, ss, rs):
        d = lax.rem(n, 2)
        q = step(place(d), 1 + 2 * w)
        src, dst = block(n, pl.ds(q * 4 + h, count), size), ring.at[n, w, pl.ds(h, count), pl.ds(0, size)]
        return copy(src, dst, ss.at[n, w], rs.at[n, w], ring_dev(d, q))

    def dir_copy(n, w, size):
        return near_copy(n, w, 2 * (1 - w), 2, size, dir_s, dir_r)

    def com_copy(n, w, size):
        return near_copy(n, w, 2 * w, 2, size, com_s, com_r)

    def all_copy(n, w, size):
        return near_copy(n, w, 0, 4, size, dir_s, dir_r)

    def sec_copy(n, k, size):
        d = lax.rem(n, 2)
        q = step(place(1 - d), k)
        src, dst = block(n, place(d) * 4 + q, size), second.at[n, k - 1, pl.ds(0, size)]
        return copy(src, dst, sec_s.at[n, k - 1], sec_r.at[n, k - 1], ring_dev(1 - d, q))

    def slabs(i):
        return len(PIECES[i]) + (i == THIRD)

    def lines(i):
        used = 24 * len(PIECES[i]) + (12 if i == THIRD else 0)
        return (used + 15) // 16 * 16

    def z_copy(i, k):
        zz = lax.rem(z + k, 8)
        size = lines(i)
        src, dst = hbuf.at[i, zz, pl.ds(0, size)], zrecv.at[i, k - 1, pl.ds(0, size)]
        return copy(src, dst, z_s.at[i, k - 1], z_r.at[i, k - 1], (zz * 4 + s, g))

    def f_copy(i, k):
        q = step(s, k)
        size = slabs(i)
        src, dst = fbuf.at[i, q, pl.ds(0, size)], frecv.at[i, k - 1, pl.ds(0, size)]
        return copy(src, dst, f_s.at[i, k - 1], f_r.at[i, k - 1], (z * 4 + q, g))

    def ma_copy(k):
        q = lax.rem(g + k, 8)
        return copy(m12.at[q], arecv.at[k - 1], ma_s.at[k - 1], ma_r.at[k - 1], (t, q))

    def mb_copy(k):
        q = lax.rem(v + k, 8)
        return copy(msg.at[q], r1.at[k - 1], mb_s.at[k - 1], mb_r.at[k - 1], (u * 8 + q, g))

    def mc_send(b):
        return copy(msg.at[8 + b], r2.at[u], mc_s.at[b], mc_r.at[u], (v * 4 + b, g))

    def mc_recv(k):
        return copy(msg.at[8], r2.at[k], mc_s.at[0], mc_r.at[k], (k * 8 + lax.div(t, 4), g))

    barrier = pltpu.get_barrier_semaphore()
    others = [ring_dev(0, step(X, 3 - 2 * xl))]
    others += [(z * 4 + step(s, k), g) for k in (1, 2, 3)]
    others += [(t, lax.rem(g + k, 8)) for k in range(1, 8)]
    others += [(lax.rem(z + k, 8) * 4 + s, g) for k in range(1, 8)]
    others += [((z + 1 - 2 * lax.rem(z, 2)) * 4 + step(s, k), g) for k in (1, 2, 3)]
    for dev in others:
        pl.semaphore_signal(barrier, inc=1, device_id=dev, device_id_type=MESH)
    for k in range(4):
        source = k * 8 + lax.div(t, 4)

        @pl.when(source != t)
        def _():
            pl.semaphore_signal(barrier, inc=1, device_id=(source, g), device_id_type=MESH)

    def columns(ref, base):
        return ref.at[:, pl.ds(pl.multiple_of(base, T), T)]

    loads = [
        (core_z, cz), (columns(core_y, v * T), cy.at[0]), (columns(core_y, (v + 1 - 2 * c) * T), cy.at[1]),
        (z_first, tz1), (z_second, tz2), (columns(y_first, v * T), ty1), (columns(y_third, v * T), ty3),
        (columns(x_second, u * T), tx2), (columns(x_third, u * T), tx3), (columns(core_x, u * T), cx),
    ]
    loads = [pltpu.make_async_copy(a, b, in_s.at[k]) for k, (a, b) in enumerate(loads)]
    own_copy(0).start()
    for load in loads:
        load.start()

    def start_own(ch, _):
        own_copy(ch).start()
        return 0

    lax.fori_loop(1, NCH, start_own, 0)

    @pl.when(lax.div(t, 4) == v)
    def _():
        pl.semaphore_wait(barrier, len(others) + 3)

    @pl.when(lax.div(t, 4) != v)
    def _():
        pl.semaphore_wait(barrier, len(others) + 4)

    par_copy(0).start()
    for load in loads[0:3]:
        load.wait()

    def r_of(row):
        h = jnp.where(row >= 48, 1, 0)
        rest = row - 48 * h
        e = rest & 15
        return 24 * (((e >> 2) & 1) * 4 + (e & 3)) + 12 * (e >> 3) + 6 * c + 3 * h + (rest >> 4)

    eye = pick(T, T, lambda row: row)
    gap = jnp.zeros((32, T), BF16)
    czt[...] = nn(pick(96, S, r_of), cz[...]).astype(BF16)
    for o in range(2):
        low, high = cy[o, 0:128], cy[o, 128:192]
        wy[0, o * T : o * T + T, :] = nt(eye, jnp.concatenate([low, high, gap, gap], axis=0)).astype(BF16)
        wy[1, o * T : o * T + T, :] = nt(eye, jnp.concatenate([low, gap, gap, high], axis=0)).astype(BF16)
    par_copy(1).start()

    def prepare():
        for load in loads[3:]:
            load.wait()
        zp[...] = nt(eye, jnp.concatenate([tz1[...], gap, tz2[...], gap], axis=0)).astype(BF16)
        y1[...] = nt(eye, jnp.concatenate([ty1[...], gap], axis=0))
        x2[...] = nt(eye, jnp.concatenate([tx2[...], gap], axis=0))
        turned = tx3[...].astype(F32)
        for n in range(T // MODE):
            x3[n, :, 0:MODE] = turned[:, n * MODE : n * MODE + MODE]
        cxp[...] = cx[...]
        fbuf[...] = jnp.zeros_like(fbuf)
        g2[...] = jnp.zeros_like(g2)
        g3[...] = jnp.zeros_like(g3)

    def contract_z(ch):
        own_copy(ch).wait()
        par_copy(ch).wait_recv()

        @pl.when(ch < NCH - 2)
        def _():
            par_copy(ch + 2).start()

        for a in range(CH):
            both = jnp.concatenate([own[ch, a], par[ch, a]], axis=0)
            w = nt(czt[...], both).astype(BF16)
            for h in range(2):
                for i in range(3):
                    at = (h * 3 + i) * 16
                    wt[h, i, ch, a * 16 : a * 16 + 16, :] = w[at : at + 16]

    def contract_y(n, k):
        ch, d, count = lax.rem(n, NCH), lax.rem(n, 2), len(PIECES[k])
        for b in range(CH // 8):
            made = {}
            for i in range(3):
                kinds = [kind for kind, index in PIECES[k] if index == i]
                if kinds:
                    first = wt[0, i, ch, b * 128 : b * 128 + 128, :]
                    other = wt[1, i, ch, b * 128 : b * 128 + 128, :]
                if kinds == [0, 1, 2]:
                    top, bot = nn(first, wy[0]), nn(other, wy[1])
                    made[0, i], made[1, i], made[2, i] = top[:, 0:128], bot[:, 0:128], top[:, 128:] + bot[:, 128:]
                elif kinds == [0, 1]:
                    made[0, i], made[1, i] = nn(first, wy[0, :, 0:128]), nn(other, wy[1, :, 0:128])
                elif kinds == [2]:
                    made[2, i] = nn(first, wy[0, :, 128:]) + nn(other, wy[1, :, 128:])
            for a in range(8):
                for m, piece in enumerate(PIECES[k]):
                    at = ((b * 8 + a) * count + m) * 16
                    us[at : at + 16, :] = made[piece][a * 16 : a * 16 + 16]
        for e in range(16):
            q = (1 - d) * e + d * ((e % 4) * 4 + e // 4)
            for m in range(count):
                lines = us[pl.ds(m * 16 + e, CH, stride=16 * count), :]
                send[n, q, m * CH : m * CH + CH, :] = lines.astype(BF16)
        if count == 1:
            opp_copy(n, CH).start()
            for w in range(2):
                all_copy(n, w, CH).start()
        else:
            for w in range(2):
                mid_copy(n, w, count * CH).start()

    def direct(n, k):
        if len(PIECES[k]) > 1:
            for w in range(2):
                dir_copy(n, w, len(PIECES[k]) * CH).start()

    def modes(n):
        ch, off = lax.div(n, 2), lax.rem(n, 2) * MODE
        rows = x2[pl.ds(pl.multiple_of(n * MODE, MODE), MODE), :]
        total = g2[...]
        factors = []
        for a in range(MODE):
            m = nn(own[ch, off + a], zp[...])
            g1[pl.ds(n * MODE + a, 1), :] = jnp.sum(m[:, 0:128] * y1[...], axis=0, keepdims=True)
            total = total + m[:, 128:] * rows[a : a + 1]
            factors.append((ty3[...].astype(F32) * x3[n, :, a : a + 1]).astype(BF16))
        g2[...] = total
        block = own[ch, pl.ds(off, MODE)].reshape(MODE * T, T)
        g3[...] += nn(jnp.concatenate(factors, axis=1), block)

    def forward(n, k):
        p, size = place(lax.rem(n, 2)), len(PIECES[k]) * CH
        if len(PIECES[k]) > 1:
            for w in range(2):
                mid_copy(n, w, size).wait_recv()
                base = step(p, 1 + 2 * w) * 4 + 2 * w
                for h in range(2):
                    mine = send[n, base + h, 0:size].astype(F32)
                    send[n, base + h, 0:size] = (mine + mid[n, 2 * w + h, 0:size].astype(F32)).astype(BF16)
                com_copy(n, w, size).start()

    def finish(n, k):
        p, size = place(lax.rem(n, 2)), len(PIECES[k]) * CH
        if len(PIECES[k]) > 1:
            for w in range(2):
                dir_copy(n, w, size).wait_recv()
                com_copy(n, w, size).wait_recv()
        else:
            opp_copy(n, size).wait_recv()
            for w in range(2):
                all_copy(n, w, size).wait_recv()
        for b in range(4):
            tot = send[n, p * 4 + b, 0:size].astype(F32) + ring[n, 0, b, 0:size].astype(F32)
            tot = tot + ring[n, 1, b, 0:size].astype(F32)
            if len(PIECES[k]) == 1:
                tot = tot + mid[n, b, 0:size].astype(F32)
            send[n, p * 4 + b, 0:size] = tot.astype(BF16)
        for o in (1, 2, 3):
            sec_copy(n, o, size).start()

    def collect(n, k):
        ch, d, size = lax.rem(n, NCH), lax.rem(n, 2), len(PIECES[k]) * CH
        for o in (1, 2, 3):
            sec_copy(n, o, size).wait_recv()
        tot = send[n, place(d) * 4 + place(1 - d), 0:size].astype(F32)
        for o in range(3):
            tot = tot + second[n, o, 0:size].astype(F32)
        tot = tot.astype(BF16)
        for m in range(len(PIECES[k])):
            gath[k, m, pl.ds(pl.multiple_of(ch * CH, CH), CH), :] = tot[m * CH : m * CH + CH]

    def drain(n, k):
        size = len(PIECES[k]) * CH
        if len(PIECES[k]) > 1:
            for w in range(2):
                mid_copy(n, w, size).wait_send()
                dir_copy(n, w, size).wait_send()
                com_copy(n, w, size).wait_send()
        else:
            opp_copy(n, size).wait_send()
            for w in range(2):
                all_copy(n, w, size).wait_send()
        for o in (1, 2, 3):
            sec_copy(n, o, size).wait_send()

    def unit(n, lag, act):
        m = n - lag

        for k in range(PARTS):

            @pl.when((m >= k * NCH) & (m < k * NCH + NCH))
            def _():
                act(m, k)

    def contract_x(i):
        parts = [nn(cxp[...], gath[i, m]).reshape(8, 24, T) for m in range(len(PIECES[i]))]
        if i == THIRD:
            parts.append(g3[...].reshape(8, 12, T))
        used = sum(p.shape[1] for p in parts)
        if used < lines(i):
            parts.append(jnp.zeros((8, lines(i) - used, T), F32))
        hbuf[i, :, 0 : lines(i), :] = jnp.concatenate(parts, axis=1).astype(BF16)
        for k in (4, 3, 5, 2, 6, 1, 7):
            z_copy(i, k).start()

    def finish_z(i):
        for k in range(1, 8):
            z_copy(i, k).wait_recv()
        tot = hbuf[i, z, 0 : lines(i), :].astype(F32)
        for k in range(7):
            tot = tot + zrecv[i, k, 0 : lines(i), :].astype(F32)
        for m in range(slabs(i)):
            each = 6 if m < len(PIECES[i]) else 3
            for q in range(4):
                at = m * 24 + q * each
                fbuf[i, q, m, 0:each] = tot[at : at + each]
        for k in (1, 2, 3):
            f_copy(i, k).start()

    def modes_a():
        high = lax.Precision.HIGHEST
        one = nn(pick(T, T, lambda q: 16 * ((q >> 1) & 7) + 2 * (q >> 4) + (q & 1), F32), g1[...], high)
        two = nn(pick(T, T, lambda q: 32 * ((q >> 2) & 3) + 4 * (q >> 4) + (q & 3), F32), g2[...], high)
        m12[:, 0:16, :] = one.reshape(8, 16, T).astype(BF16)
        m12[:, 16:32, :] = two.reshape(8, 16, T).astype(BF16)
        for k in range(1, 8):
            ma_copy(k).start()

    def modes_b():
        total = m12[g].astype(F32)
        for k in range(1, 8):
            ma_copy(k).wait_recv()
            total = total + arecv[k - 1].astype(F32)

        def source_row(q):
            i = q & 7
            low = jnp.where(i < 2, 2 * (q >> 3) + i, -1)
            return jnp.where(q < 64, low, jnp.where(i < 4, 16 + 4 * ((q - 64) >> 3) + i, -1))

        msg[...] = nn(pick(96, 32, source_row, F32), total, lax.Precision.HIGHEST).reshape(12, 8, T)
        for k in range(1, 8):
            mb_copy(k).start()
        for b in range(4):

            @pl.when(v * 4 + b != t)
            def _():
                mc_send(b).start()

            @pl.when(v * 4 + b == t)
            def _():
                r2[u] = msg[8 + b]

    def turn(n, _):
        @pl.when(n < NCH)
        def _():
            contract_z(n)

        @pl.when(n == MODE_0 - 1)
        def _():
            prepare()

        unit(n, 0, contract_y)
        unit(n, DIRECT, direct)
        unit(n, FORWARD, forward)

        unit(n, FINISH, finish)
        unit(n, COLLECT, collect)

        @pl.when((n >= MODE_0) & (n < MODE_0 + T // MODE))
        def _():
            modes(n - MODE_0)

        for i in range(PARTS):
            last = NCH * i + NCH - 1 + COLLECT

            @pl.when(n == last)
            def _():
                contract_x(i)

            if last + ZLAG < UNITS + COLLECT:

                @pl.when(n == last + ZLAG)
                def _():
                    finish_z(i)

        @pl.when(n == MODE_A)
        def _():
            modes_a()

        @pl.when(n == MODE_B)
        def _():
            modes_b()

        return 0

    lax.fori_loop(0, UNITS + COLLECT, turn, 0)

    def sent(n, _):
        unit(n, 0, drain)
        return 0

    lax.fori_loop(0, UNITS, sent, 0)
    for ch in range(NCH):
        par_copy(ch).wait_send()
    for k in range(1, 8):
        ma_copy(k).wait_send()

    def place_rows(i):
        for m, (kind, index) in enumerate(PIECES[i]):
            out[s * 9 + kind * 3 + index] = fbuf[i, s, m]
        for k in (1, 2, 3):
            f_copy(i, k).wait_recv()
            for m, (kind, index) in enumerate(PIECES[i]):
                out[step(s, 4 - k) * 9 + kind * 3 + index] = frecv[i, k - 1, m]
        if i == THIRD:
            at = len(PIECES[i])
            out[36] = fbuf[i, s, at] + frecv[i, 0, at] + frecv[i, 1, at] + frecv[i, 2, at]

    def drain_rows(i):
        for k in range(1, 8):
            z_copy(i, k).wait_send()
        for k in (1, 2, 3):
            f_copy(i, k).wait_send()

    for i in range(PARTS - 1):
        if NCH * i + NCH - 1 + ZLAG >= UNITS:
            finish_z(i)

    first = msg[v]
    for k in range(1, 8):
        mb_copy(k).wait_recv()
        first = first + r1[k - 1]
    out[37] = first
    for k in range(4):

        @pl.when(k * 8 + lax.div(t, 4) != t)
        def _():
            mc_recv(k).wait_recv()

    out[38] = r2[0] + r2[1] + r2[2] + r2[3]
    for k in range(1, 8):
        mb_copy(k).wait_send()
    for b in range(4):

        @pl.when(v * 4 + b != t)
        def _():
            mc_send(b).wait_send()

    for i in range(PARTS - 1):
        place_rows(i)
        drain_rows(i)
    finish_z(PARTS - 1)
    place_rows(PARTS - 1)
    drain_rows(PARTS - 1)


def outputs_kernel(x, one, two, three, core):
    one[...] = x[37 * 8 : 37 * 8 + 2, 0:K]
    two[...] = x[38 * 8 : 38 * 8 + 4, 0:K]
    three[...] = x[36 * 8 : 36 * 8 + 3, :]
    for p in range(6):
        rows = x[pl.ds(p, 36, stride=8), :]
        for q in range(4):
            core[p, 6 * q : 6 * q + 6, 0:128] = rows[9 * q : 9 * q + 6]
            core[p, 6 * q : 6 * q + 3, 128:192] = rows[9 * q + 6 : 9 * q + 9, 0:64]
            core[p, 6 * q + 3 : 6 * q + 6, 128:192] = rows[9 * q + 6 : 9 * q + 9, 64:128]


def shards(field, *small):
    vm, hbm = pl.BlockSpec(memory_space=pltpu.VMEM), pl.BlockSpec(memory_space=pl.ANY)
    dma, mem = pltpu.SemaphoreType.DMA, pltpu.VMEM
    unit = [dma((UNITS, 2))] * 6 + [dma((UNITS, 3))] * 2
    raw = pl.pallas_call(
        main_kernel,
        out_shape=jax.ShapeDtypeStruct((39, 8, 128), F32),
        in_specs=[hbm] * 10,
        out_specs=vm,
        scratch_shapes=[
            mem((NCH, CH, T, T), BF16),
            mem((NCH, CH, T, T), BF16),
            mem((2, 3, NCH, CH * 16, 256), BF16),
            mem((CH * 16 * MOST, 128), F32),
            mem((UNITS, 16, ROWS, 128), BF16),
            mem((UNITS, 4, ROWS, 128), BF16),
            mem((UNITS, 2, 4, ROWS, 128), BF16),
            mem((UNITS, 3, ROWS, 128), BF16),
            mem((PARTS, MOST, T, 128), BF16),
            mem((PARTS, 8, 32 * MOST + 32, 128), BF16),
            mem((PARTS, 7, 32 * MOST + 32, 128), BF16),
            mem((PARTS, 4, MOST + 1, 8, 128), F32),
            mem((PARTS, 3, MOST + 1, 8, 128), F32),
            mem((S, T), BF16), mem((2, S, T), BF16), mem((S, T), BF16),
            mem((K, T), BF16), mem((K, T), BF16), mem((K, T), BF16), mem((K, T), BF16),
            mem((K, T), BF16), mem((K, T), BF16),
            mem((K, T), BF16),
            mem((S, T), BF16),
            mem((2, 2 * T, 256), BF16),
            mem((T, 256), BF16),
            mem((T, 128), F32), mem((T, 128), F32),
            mem((T // MODE, K, 128), F32),
            mem((T, 128), F32), mem((T, 128), F32), mem((K, T), F32),
            mem((8, 32, 128), BF16), mem((7, 32, 128), BF16),
            mem((12, 8, 128), F32), mem((7, 8, 128), F32), mem((4, 8, 128), F32),
            dma((10,)), dma((NCH,)), dma((NCH,)), dma((NCH,)),
            *unit,
            dma((PARTS, 7)), dma((PARTS, 7)), dma((PARTS, 3)), dma((PARTS, 3)),
            dma((7,)), dma((7,)), dma((7,)), dma((7,)), dma((4,)), dma((4,)),
        ],
        compiler_params=pltpu.CompilerParams(
            collective_id=0, has_side_effects=True, vmem_limit_bytes=56 * 1024 * 1024
        ),
    )(field, *[x.T for x in small])
    one, two, three, core = pl.pallas_call(
        outputs_kernel,
        out_shape=(
            jax.ShapeDtypeStruct((2, K), F32),
            jax.ShapeDtypeStruct((4, K), F32),
            jax.ShapeDtypeStruct((3, T), F32),
            jax.ShapeDtypeStruct((6, 24, S), F32),
        ),
        in_specs=[vm],
        out_specs=(vm, vm, vm, vm),
    )(raw.reshape(39 * 8, 128))
    return (one, two, three, core.transpose(0, 2, 1))


def solution(mesh):
    return jax.shard_map(
        shards,
        mesh=mesh,
        in_specs=(
            P("xy", None, None, "gz"),
            P(), P(), P("gz", None), P(), P(), P(), P(), P("gz", None), P("gz", None),
        ),
        out_specs=(
            P(("xy", "gz"), None),
            P(("xy", "gz"), None),
            P("xy", "gz"),
            P("xy", None, "gz"),
        ),
        check_vma=False,
    )
```
